768 devices in a mesh: tile: 24 (over x_lo, z), slab: 32 (over x_hi, y, core).
Axes of the slice: x: 4 (x_hi: 2, x_lo: 2; x = x_hi * 2 + x_lo), y: 8, z: 12, core: 2. Of those that a mesh axis runs over, the one named last changes fastest.
Arguments:
- newton_step: float32 [10, 3072, 4096], P(None, 'tile', 'slab'), may hold values from -6 to 6
- suction: float32 [10, 3072, 4096], P(None, 'tile', 'slab'), may hold values from 0.2 to 2
- conductivity: float32 [10, 3072, 4096], P(None, 'tile', 'slab'), may hold values from 0.1 to 10
- vg_alpha: float32 [10, 3072, 4096], P(None, 'tile', 'slab'), may hold values from 0.5 to 2
- porosity: float32 [10, 3072, 4096], P(None, 'tile', 'slab'), may hold values from 0.2 to 0.5
- ponded: float32 [3072, 4096], P(('tile', 'slab')), may hold values from 0.05 to 1
- slope_x: float32 [3072, 4096], P(('tile', 'slab')), may hold values from 0.001 to 0.1
- slope_y: float32 [3072, 4096], P(('tile', 'slab')), may hold values from 0.001 to 0.1
- manning: float32 [3072, 4096], P(('tile', 'slab')), may hold values from 0.03 to 0.3
- river_mask: int32 [3072, 4096], P(('tile', 'slab')), may hold values 0 or 1
- slope_code: int32 [3072, 4096], P(('tile', 'slab')), may hold values from 0 to 3
Outputs:
- subsurface_jv: float32 [10, 3072, 4096], P(None, 'tile', 'slab')
- surface_jv: float32 [3072, 4096], P(('tile', 'slab'))
The draws below stay inside these ranges and needn't reach their ends.
Inputs may be any that keep to these rules, and one draw needn't show every extreme that they name: `river_mask`: river cells are those with value 1. `slope_code`: bit 0 picks the row direction and bit 1 the column direction of downslope routing.
All inputs are finite; a program needn't handle non-finite values. No bound on the sum of `river_mask` on one device may be relied on, other than what follows from the above.
Results may differ from the reference program's by a relative error of at most 0.0003.
Values sent between devices are 32-bit elements; how exact they have to be, the bound alone decides.
A program may use at most 64 MiB of HBM per device.

```python
import math
import jax
import jax.numpy as jnp
from jax import lax

NZ = 10
NX = 3072
NY = 4096


def set_ends(result, key, least, high):
    dims = result.shape
    place = [jax.random.randint(jax.random.fold_in(key, axis), (), 0, dims[axis]) for axis in range(len(dims))]
    result = result.at[tuple(place)].set(least)
    longest = dims.index(max(dims))
    place[longest] = (place[longest] + 1) % dims[longest]
    return result.at[tuple(place)].set(high)


def level_of(rng, dims, shards, low, largest):
    def one(position, shards_of):
        heights = jax.random.uniform(jax.random.fold_in(jax.random.fold_in(rng, 6), position), (shards_of,), jnp.float32, low / len(shards), largest / len(shards))
        return jnp.repeat(jnp.exp(heights), dims[position] // shards_of).reshape((-1,) + (1,) * (len(dims) - position - 1))

    gain = one(*shards[0])
    for cut in shards[1:]:
        gain = gain * one(*cut)
    return gain


def noise(rng, dims, width, limit, split=(), kind=jnp.bfloat16):
    result = jax.random.normal(rng, dims, jnp.float32) * width
    if len(split) > 0:
        result = level_of(rng, dims, split, -0.22, 0.18) * result
    return jnp.clip(result, min=-limit, max=limit).astype(kind)


def setup_inputs(seed: int = 0) -> dict:
    seeds = jax.random.split(jax.random.key(seed), 12)
    return {
        "newton_step": noise(seeds[0], (NZ, NX, NY), 1.0, 6.0, ((1, 24), (2, 32)), jnp.float32),
        "suction": jnp.clip(jnp.exp(math.log(2.0) - 2.3025851 * jax.random.uniform(seeds[1], (NZ, NX, NY), jnp.float32) ** level_of(seeds[1], (NZ, NX, NY), ((1, 24), (2, 32)), -0.2, 0.2)), 0.2, 2.0),
        "conductivity": jnp.clip(jnp.exp(math.log(10.0) - 4.6051702 * jax.random.uniform(seeds[2], (NZ, NX, NY), jnp.float32) ** level_of(seeds[2], (NZ, NX, NY), ((1, 24), (2, 32)), -0.2, 0.2)), 0.1, 10.0),
        "vg_alpha": jnp.clip(jnp.exp(math.log(2.0) - 1.3862944 * jax.random.uniform(seeds[3], (NZ, NX, NY), jnp.float32) ** level_of(seeds[3], (NZ, NX, NY), ((1, 24), (2, 32)), -0.2, 0.2)), 0.5, 2.0),
        "porosity": jnp.clip(0.2 + 0.3 * jax.random.uniform(seeds[4], (NZ, NX, NY), jnp.float32) ** level_of(seeds[4], (NZ, NX, NY), ((1, 24), (2, 32)), -0.2, 0.2), 0.2, 0.5),
        "ponded": jnp.clip(jnp.exp(math.log(1.0) - 2.9957323 * jax.random.uniform(seeds[5], (NX, NY), jnp.float32) ** level_of(seeds[5], (NX, NY), ((0, 768),), -0.2, 0.2)), 0.05, 1.0),
        "slope_x": jnp.clip(jnp.exp(math.log(0.1) - 4.6051702 * jax.random.uniform(seeds[6], (NX, NY), jnp.float32) ** level_of(seeds[6], (NX, NY), ((0, 768),), -0.2, 0.2)), 0.001, 0.1),
        "slope_y": jnp.clip(jnp.exp(math.log(0.1) - 4.6051702 * jax.random.uniform(seeds[7], (NX, NY), jnp.float32) ** level_of(seeds[7], (NX, NY), ((0, 768),), -0.2, 0.2)), 0.001, 0.1),
        "manning": jnp.clip(jnp.exp(math.log(0.3) - 2.3025852 * jax.random.uniform(seeds[8], (NX, NY), jnp.float32) ** level_of(seeds[8], (NX, NY), ((0, 768),), -0.2, 0.2)), 0.03, 0.3),
        "river_mask": set_ends((jax.random.randint(seeds[9], (NX, NY), 0, 5) < 2).astype(jnp.int32), jax.random.fold_in(seeds[9], 1), 0, 1),
        "slope_code": set_ends(jax.random.randint(seeds[10], (NX, NY), 0, 4), jax.random.fold_in(seeds[10], 1), 0, 3).astype(jnp.int32),
    }


specific_storage = 0.01

def retention(suction, vg_alpha):
    scaled = (vg_alpha * suction) ** 2
    one_plus = 1.0 + scaled
    saturation = one_plus ** (-0.5)
    root_w = jnp.sqrt(scaled / one_plus)
    bracket = 1.0 - root_w
    quarter = one_plus ** (-0.25)
    rel_perm = quarter * bracket * bracket
    slope_u = -0.25 * quarter / one_plus * bracket * bracket - quarter * bracket / (root_w * one_plus * one_plus)
    rel_deriv = -slope_u * 2.0 * scaled / suction
    sat_deriv = scaled * one_plus ** (-1.5) / suction
    return (saturation, rel_perm, rel_deriv, sat_deriv)

def cell_state(newton_step, suction, conductivity, vg_alpha, porosity):
    saturation, rel_perm, rel_deriv, sat_deriv = retention(suction, vg_alpha)
    storage = (specific_storage * saturation + porosity * sat_deriv) * newton_step
    stacked = jnp.stack([newton_step, -suction, conductivity * rel_perm, conductivity * rel_deriv * newton_step])
    return (stacked, storage)

def face_term(center, beside, gravity):
    return 0.5 * (center[2] + beside[2]) * (center[0] - beside[0]) + 0.5 * (center[3] + beside[3]) * (center[1] - beside[1] + gravity)

def neighbour_pair(values, axis_dim):
    length = values.shape[axis_dim]
    zeros_rim = jnp.zeros_like(lax.slice_in_dim(values, 0, 1, axis=axis_dim))
    previous = jnp.concatenate([zeros_rim, lax.slice_in_dim(values, 0, length - 1, axis=axis_dim)], axis_dim)
    following = jnp.concatenate([lax.slice_in_dim(values, 1, length, axis=axis_dim), zeros_rim], axis_dim)
    return (previous, following)

def surface_terms(top_step, ponded, slope_x, slope_y, manning, river_mask, slope_code):
    conveyance = 5.0 / 3.0 * ponded ** (2.0 / 3.0) / manning * top_step
    across = jnp.where(river_mask == 1, 0.0, conveyance * jnp.sqrt(slope_x))
    lateral = conveyance * jnp.sqrt(slope_y)
    plus_rows = jnp.where(slope_code % 2 == 1, across, 0.0)
    minus_rows = across - plus_rows
    plus_cols = jnp.where(slope_code // 2 == 1, lateral, 0.0)
    minus_cols = lateral - plus_cols
    return (plus_rows, minus_rows, plus_cols, minus_cols, across + lateral)

def reference(newton_step, suction, conductivity, vg_alpha, porosity, ponded, slope_x, slope_y, manning, river_mask, slope_code):
    layers = newton_step.shape[0]
    fields = (newton_step, suction, conductivity, vg_alpha, porosity)

    def layer_at(layer_index):
        inside = (layer_index >= 0) & (layer_index < layers)
        clamped = jnp.clip(layer_index, 0, layers - 1).astype(jnp.int32)
        pieces = [lax.dynamic_index_in_dim(array, clamped, 0, keepdims=False) for array in fields]
        stacked, storage = cell_state(*pieces)
        return (jnp.where(inside, stacked, jnp.zeros_like(stacked)), storage)

    def one_layer(layer_index):
        center, storage = layer_at(layer_index)
        upward, unused_one = layer_at(layer_index - 1)
        downward, unused_two = layer_at(layer_index + 1)
        summed = storage + face_term(center, upward, -1.0) + face_term(center, downward, 1.0)
        for axis_dim in (1, 2):
            previous, following = neighbour_pair(center, axis_dim)
            summed = summed + face_term(center, previous, 0.0) + face_term(center, following, 0.0)
        return summed
    subsurface_jv = lax.map(one_layer, jnp.arange(layers, dtype=jnp.int32))
    plus_rows, minus_rows, plus_cols, minus_cols, outflow = surface_terms(newton_step[0], ponded, slope_x, slope_y, manning, river_mask, slope_code)
    inflow = neighbour_pair(plus_rows, 0)[0] + neighbour_pair(minus_rows, 0)[1]
    inflow = inflow + neighbour_pair(plus_cols, 1)[0] + neighbour_pair(minus_cols, 1)[1]
    return (subsurface_jv, outflow - inflow)
```

```python
import functools

import jax
import jax.numpy as jnp
from jax import lax
from jax.experimental import pallas as pl
from jax.experimental.pallas import tpu as pltpu
from jax.sharding import PartitionSpec as P

MESH = pl.DeviceIdType.MESH
W = 128
specific_storage = 0.01


def relative(suction, vg_alpha):
    w = vg_alpha * suction
    saturation = lax.rsqrt(1.0 + w * w)
    quarter = saturation * lax.rsqrt(saturation)
    bracket = 1.0 - w * saturation
    return w, saturation, quarter, bracket


def half_state(v, suction, conductivity, vg_alpha):
    w, saturation, quarter, bracket = relative(suction, vg_alpha)
    kb = conductivity * quarter * bracket
    m = vg_alpha * saturation * saturation
    a = 0.5 * kb * bracket
    b = kb * m * (0.25 * bracket * w + saturation) * v
    return a, b, w * m * saturation, saturation


def face(v, s, a, b, vj, sj, aj, bj):
    return (a + aj) * (v - vj) + (b + bj) * (sj - s)


def kernel(
    nt,
    ns,
    nz,
    H,
    R,
    v_h,
    s_h,
    k_h,
    al_h,
    ph_h,
    pond_h,
    sx_h,
    sy_h,
    man_h,
    riv_h,
    code_h,
    out_h,
    surf_h,
    v_s,
    s_s,
    k_s,
    al_s,
    ph_s,
    sa,
    sb,
    out_s,
    pond,
    sx,
    sy,
    man,
    riv,
    code,
    surf_s,
    c_all,
    c_xp,
    c_xm,
    c_yp,
    c_ym,
    top_stage,
    rtop,
    rim_stage,
    rim,
    cp_stage,
    cm_stage,
    rcp,
    rcm,
    row_up,
    row_dn,
    rrow_up,
    rrow_dn,
    col_l,
    col_r,
    rcol_l,
    rcol_r,
    pt,
    ft,
    load_sem,
    store_sem,
    top_send,
    top_recv,
    rim_send,
    rim_recv,
    cf_send,
    cf_recv,
    halo_send,
    halo_recv,
):
    t = lax.axis_index("tile")
    s = lax.axis_index("slab")
    t_prev, t_next = lax.rem(t + nt - 1, nt), lax.rem(t + 1, nt)
    s_prev, s_next = lax.rem(s + ns - 1, ns), lax.rem(s + 1, ns)
    o_prev_t = jnp.where(s == 0, t_prev, t)
    o_next_t = jnp.where(s == ns - 1, t_next, t)

    inside = pl.ds(1, nz)
    loads = []
    for i, (src, dst) in enumerate(
        [
            (v_h, v_s.at[inside]),
            (s_h, s_s.at[inside]),
            (k_h, k_s),
            (al_h, al_s),
            (pond_h, pond),
            (sx_h, sx),
            (sy_h, sy),
            (man_h, man),
            (riv_h, riv),
            (code_h, code),
            (ph_h, ph_s),
        ]
    ):
        copy = pltpu.make_async_copy(src, dst, load_sem.at[i])
        copy.start()
        loads.append(copy)

    barrier = pltpu.get_barrier_semaphore()

    def greet(tt, ss):
        pl.semaphore_signal(barrier, inc=1, device_id=(tt, ss), device_id_type=MESH)

    @pl.when(s == 0)
    def _():
        @pl.loop(1, ns)
        def _(d):
            greet(t_prev, d)

    @pl.when(s == ns - 1)
    def _():
        @pl.loop(0, ns - 1)
        def _(d):
            greet(t_next, d)

    greet(t_prev, s)
    greet(t_next, s)

    @pl.loop(1, ns)
    def _(d):
        greet(t, lax.rem(s + d, ns))

    zero = jnp.zeros((H, W), jnp.float32)
    for ref in (v_s, s_s, sa, sb):
        ref[0] = zero
        ref[nz + 1] = zero

    loads[0].wait()
    for j in range(ns):
        lo, hi = max(R * j - 1, 0), min(R * j + R + 1, H)
        at = lo - (R * j - 1)
        top_stage[j, at : at + hi - lo, :] = v_s[1, lo:hi, :]
    rim_stage[0] = v_s[1, H - 1 : H, :]
    rim_stage[1] = v_s[1, 0:1, :]

    lane = lax.broadcasted_iota(jnp.int32, (8, W), 1)
    sub = lax.broadcasted_iota(jnp.int32, (8, W), 0)
    pair = lax.shift_right_logical(lane, 1)
    fields = ((v_s, 1), (s_s, 1), (k_s, 0), (al_s, 0))
    edges = [jnp.zeros((8, W), jnp.float32) for _ in range(H // 8)]
    for f, (ref, first) in enumerate(fields):
        if f > 0:
            loads[f].wait()
        for layer in range(nz):
            k = f * nz + layer
            row_up[k : k + 1, :] = ref[layer + first, 0:1, :]
            row_dn[k : k + 1, :] = ref[layer + first, H - 1 : H, :]
            here = pair == k
            for c in range(H // 8):
                x = ref[layer + first, c * 8 : c * 8 + 8, :]
                edges[c] = jnp.where(here, pltpu.roll(x, 2 * k + 1, 1), edges[c])
    pt[...] = jnp.concatenate(edges, axis=0).T
    col_l[...] = pt[pl.ds(1, 4 * nz, stride=2), :]
    col_r[...] = pt[pl.ds(0, 4 * nz, stride=2), :]

    for i in range(4, 10):
        loads[i].wait()
    for j in range(ns):
        cols = slice(j * W, j * W + W)
        g = (5.0 / 3.0) * jnp.exp((2.0 / 3.0) * jnp.log(pond[:, cols])) / man[:, cols]
        x, y = sx[:, cols], sy[:, cols]
        cx = jnp.where(riv[:, cols] == 1, 0.0, g * (x * lax.rsqrt(x)))
        cy = g * (y * lax.rsqrt(y))
        bits = code[:, cols]
        xp = jnp.where((bits & 1) == 1, cx, 0.0)
        xm = cx - xp
        yp = jnp.where(lax.shift_right_logical(bits, 1) == 1, cy, 0.0)
        c_all[j] = cx + cy
        c_xp[j, 1:R, :] = xp[0 : R - 1]
        c_xm[j, 0 : R - 1, :] = xm[1:R]
        c_yp[j] = yp
        c_ym[j] = cy - yp
        cp_stage[j] = xp[R - 1 : R]
        cm_stage[j] = xm[0:1]

    pl.semaphore_wait(
        barrier, ns + 1 + jnp.where(s == 0, 0, 1) + jnp.where(s == ns - 1, 0, 1)
    )

    def send(src, dst, send_sem, recv_sem, tt, ss):
        return pltpu.make_async_remote_copy(
            src_ref=src,
            dst_ref=dst,
            send_sem=send_sem,
            recv_sem=recv_sem,
            device_id=(tt, ss),
            device_id_type=MESH,
        )

    halos = [
        send(row_up, rrow_dn, halo_send.at[0], halo_recv.at[0], t_prev, s),
        send(row_dn, rrow_up, halo_send.at[1], halo_recv.at[1], t_next, s),
        send(col_l, rcol_r, halo_send.at[2], halo_recv.at[2], t, s_prev),
        send(col_r, rcol_l, halo_send.at[3], halo_recv.at[3], t, s_next),
    ]
    coefs = [
        send(cp_stage, rcp, cf_send.at[0], cf_recv.at[0], o_next_t, s_next),
        send(cm_stage, rcm, cf_send.at[1], cf_recv.at[1], o_prev_t, s_prev),
    ]
    rims = [
        send(rim_stage.at[0], rim.at[s], rim_send.at[0], rim_recv.at[s], t_next, 0),
        send(rim_stage.at[1], rim.at[s], rim_send.at[1], rim_recv.at[s], t_prev, ns - 1),
    ]

    def top_copy(d):
        peer = lax.rem(s + d, ns)
        return send(
            top_stage.at[peer], rtop.at[s], top_send.at[d], top_recv.at[s], t, peer
        )

    for copy in halos + coefs:
        copy.start()

    @pl.loop(1, ns)
    def _(d):
        top_copy(d).start()

    for copy in rims:
        copy.start()
    rtop[s] = top_stage[s]

    loads[10].wait()
    inner_lane = lane < W - 1
    first_row = sub == 0

    @pl.loop(0, nz)
    def _(layer):
        lp = layer + 1
        for c in range(H // 8):
            rows = slice(c * 8, c * 8 + 8)
            v = v_s[lp, rows, :]
            a, b, sat_deriv, saturation = half_state(
                v, s_s[lp, rows, :], k_s[layer, rows, :], al_s[layer, rows, :]
            )
            sa[lp, rows, :] = a
            sb[lp, rows, :] = b
            out_s[lp, rows, :] = (
                specific_storage * saturation + ph_s[layer, rows, :] * sat_deriv
            ) * v
        carried = jnp.zeros((8, W), jnp.float32)
        for c in range(H // 8):
            rows = slice(c * 8, c * 8 + 8)
            here = [ref[lp, rows, :] for ref in (v_s, s_s, sa, sb)]
            beside = [pltpu.roll(x, W - 1, 1) for x in here]
            flux = jnp.where(inner_lane, face(*here, *beside), 0.0)
            total = out_s[lp, rows, :] + flux - pltpu.roll(flux, 1, 1)
            if c < H // 8 - 1:
                after = slice(c * 8 + 1, c * 8 + 9)
                flux = face(*here, *[ref[lp, after, :] for ref in (v_s, s_s, sa, sb)])
            else:
                flux = jnp.where(sub == 7, 0.0, face(*here, *[pltpu.roll(x, 7, 0) for x in here]))
            shifted = pltpu.roll(flux, 1, 0)
            total = total + flux - jnp.where(first_row, carried, shifted)
            carried = shifted
            v, suction, a, b = here
            above = [ref[layer, rows, :] for ref in (v_s, s_s, sa, sb)]
            flux = (a + above[2]) * (above[0] - v) + (b + above[3]) * (suction - above[1] + 1.0)
            out_s[layer, rows, :] = out_s[layer, rows, :] + flux
            out_s[lp, rows, :] = total - flux

    for c in range(H // 8):
        rows = slice(c * 8, c * 8 + 8)
        out_s[nz, rows, :] = (
            out_s[nz, rows, :]
            + sa[nz, rows, :] * v_s[nz, rows, :]
            + sb[nz, rows, :] * (1.0 - s_s[nz, rows, :])
        )

    def parts(ref):
        return [ref[f * nz : f * nz + nz, :] for f in range(4)]

    def edge_state(raw):
        a, b, _, _ = half_state(*raw)
        return raw[0], raw[1], a, b

    def outside(exists, raw):
        return [jnp.where(exists, x, 0.0) for x in edge_state(raw)]

    for copy in halos:
        copy.wait_recv()
    ft[...] = jnp.zeros(ft.shape, jnp.float32)
    ft[pl.ds(1, nz, stride=2), :] = face(
        *edge_state(parts(col_l)), *outside(s > 0, parts(rcol_l))
    )
    ft[pl.ds(0, nz, stride=2), :] = face(
        *edge_state(parts(col_r)), *outside(s < ns - 1, parts(rcol_r))
    )
    up = face(*edge_state(parts(row_up)), *outside(t > 0, parts(rrow_up)))
    down = face(*edge_state(parts(row_dn)), *outside(t < nt - 1, parts(rrow_dn)))
    for layer in range(nz):
        out_s[layer + 1, 0:1, :] = out_s[layer + 1, 0:1, :] + up[layer : layer + 1]
        out_s[layer + 1, H - 1 : H, :] = out_s[layer + 1, H - 1 : H, :] + down[layer : layer + 1]
    turned = ft[...].T
    rim_lane = (lane == 0) | (lane == W - 1)
    for layer in range(nz):
        for c in range(H // 8):
            rows = slice(c * 8, c * 8 + 8)
            x = pltpu.roll(turned[rows], W - (2 * layer + 1), 1)
            out_s[layer + 1, rows, :] = out_s[layer + 1, rows, :] + jnp.where(rim_lane, x, 0.0)
    out_copy = pltpu.make_async_copy(out_s.at[inside], out_h, store_sem.at[0])
    out_copy.start()

    for copy in coefs:
        copy.wait_recv()

    @pl.loop(1, ns)
    def _(d):
        peer = lax.rem(s + d, ns)
        send(
            top_stage.at[peer], rtop.at[peer], top_send.at[d], top_recv.at[peer], t, peer
        ).wait_recv()

    def rim_wait():
        @pl.loop(0, ns)
        def _(j):
            send(rim_stage.at[0], rim.at[j], rim_send.at[0], rim_recv.at[j], t_next, 0).wait_recv()

    @pl.when(s == 0)
    def _():
        rim_wait()
        for j in range(ns):
            rtop[j, 0:1, :] = rim[j]

    @pl.when(s == ns - 1)
    def _():
        rim_wait()
        for j in range(ns):
            rtop[j, R + 1 : R + 2, :] = rim[j]

    has_prev = (t > 0) | (s > 0)
    has_next = (t < nt - 1) | (s < ns - 1)
    small_lane = lax.broadcasted_iota(jnp.int32, (R, W), 1)
    first, last = small_lane == 0, small_lane == W - 1
    nil = jnp.zeros((R, W), jnp.float32)
    prev_plus = nil
    tops = [rtop[j, 1 : R + 1, :] for j in range(ns)]
    minus = [pltpu.roll(c_ym[j] * tops[j], W - 1, 1) for j in range(ns)] + [nil]
    for j in range(ns):
        c_xp[j, 0:1, :] = jnp.where(has_prev, rcp[j], 0.0)
        c_xm[j, R - 1 : R, :] = jnp.where(has_next, rcm[j], 0.0)
        plus = pltpu.roll(c_yp[j] * tops[j], 1, 1)
        surf_s[:, j * W : j * W + W] = (
            c_all[j] * tops[j]
            - c_xp[j] * rtop[j, 0:R, :]
            - c_xm[j] * rtop[j, 2 : R + 2, :]
            - jnp.where(first, prev_plus, plus)
            - jnp.where(last, minus[j + 1], minus[j])
        )
        prev_plus = plus
    surf_copy = pltpu.make_async_copy(surf_s, surf_h, store_sem.at[1])
    surf_copy.start()

    for copy in halos + coefs + rims:
        copy.wait_send()

    @pl.loop(1, ns)
    def _(d):
        top_copy(d).wait_send()

    out_copy.wait()
    surf_copy.wait()


def per_device(nt, ns, *args):
    nz, H, _ = args[0].shape
    R = args[5].shape[0]
    f32 = jnp.float32
    vm = pltpu.VMEM
    dma = pltpu.SemaphoreType.DMA
    anywhere = pl.BlockSpec(memory_space=pl.ANY)
    return pl.pallas_call(
        functools.partial(kernel, nt, ns, nz, H, R),
        out_shape=(
            jax.ShapeDtypeStruct((nz, H, W), f32),
            jax.ShapeDtypeStruct((R, ns * W), f32),
        ),
        in_specs=[anywhere] * 11,
        out_specs=(anywhere, anywhere),
        scratch_shapes=[
            vm((nz + 2, H, W), f32),
            vm((nz + 2, H, W), f32),
            vm((nz, H, W), f32),
            vm((nz, H, W), f32),
            vm((nz, H, W), f32),
            vm((nz + 2, H, W), f32),
            vm((nz + 2, H, W), f32),
            vm((nz + 1, H, W), f32),
            vm((R, ns * W), f32),
            vm((R, ns * W), f32),
            vm((R, ns * W), f32),
            vm((R, ns * W), f32),
            vm((R, ns * W), jnp.int32),
            vm((R, ns * W), jnp.int32),
            vm((R, ns * W), f32),
            vm((ns, R, W), f32),
            vm((ns, R, W), f32),
            vm((ns, R, W), f32),
            vm((ns, R, W), f32),
            vm((ns, R, W), f32),
            vm((ns, R + 2, W), f32),
            vm((ns, R + 2, W), f32),
            vm((2, 1, W), f32),
            vm((ns, 1, W), f32),
            vm((ns, 1, W), f32),
            vm((ns, 1, W), f32),
            vm((ns, 1, W), f32),
            vm((ns, 1, W), f32),
            vm((4 * nz, W), f32),
            vm((4 * nz, W), f32),
            vm((4 * nz, W), f32),
            vm((4 * nz, W), f32),
            vm((4 * nz, H), f32),
            vm((4 * nz, H), f32),
            vm((4 * nz, H), f32),
            vm((4 * nz, H), f32),
            vm((W, H), f32),
            vm((W, H), f32),
            dma((11,)),
            dma((2,)),
            dma((ns,)),
            dma((ns,)),
            dma((2,)),
            dma((ns,)),
            dma((2,)),
            dma((2,)),
            dma((4,)),
            dma((4,)),
        ],
        compiler_params=pltpu.CompilerParams(
            collective_id=0, has_side_effects=True, vmem_limit_bytes=56 * 1024 * 1024
        ),
    )(*args)


def solution(mesh):
    cells = P(None, "tile", "slab")
    surface = P(("tile", "slab"), None)
    return jax.shard_map(
        functools.partial(per_device, mesh.shape["tile"], mesh.shape["slab"]),
        mesh=mesh,
        in_specs=(cells,) * 5 + (surface,) * 6,
        out_specs=(cells, surface),
        check_vma=False,
    )
```

```python
import functools

import jax
import jax.numpy as jnp
from jax import lax
from jax.experimental import pallas as pl
from jax.experimental.pallas import tpu as pltpu
from jax.sharding import PartitionSpec as P

MESH = pl.DeviceIdType.MESH
W = 128
specific_storage = 0.01


def relative(suction, vg_alpha):
    w = vg_alpha * suction
    saturation = lax.rsqrt(1.0 + w * w)
    quarter = saturation * lax.rsqrt(saturation)
    bracket = 1.0 - w * saturation
    return w, saturation, quarter, bracket


def half_state(v, suction, conductivity, vg_alpha):
    w, saturation, quarter, bracket = relative(suction, vg_alpha)
    kb = conductivity * quarter * bracket
    m = vg_alpha * saturation * saturation
    a = 0.5 * kb * bracket
    b = kb * m * (0.25 * bracket * w + saturation) * v
    return a, b, w * m * saturation, saturation


def face(v, s, a, b, vj, sj, aj, bj):
    return (a + aj) * (v - vj) + (b + bj) * (sj - s)


def kernel(
    nt,
    ns,
    nz,
    H,
    R,
    v_h,
    s_h,
    k_h,
    al_h,
    ph_h,
    pond_h,
    sx_h,
    sy_h,
    man_h,
    riv_h,
    code_h,
    out,
    surf,
    v_s,
    s_s,
    k_s,
    al_s,
    ph_s,
    sa,
    sb,
    pond,
    sx,
    sy,
    man,
    riv,
    code,
    c_all,
    c_xp,
    c_xm,
    c_yp,
    c_ym,
    top_stage,
    mid,
    rtop,
    cp_stage,
    cm_stage,
    rcp,
    rcm,
    row_up,
    row_dn,
    rrow_up,
    rrow_dn,
    col_l,
    col_r,
    rcol_l,
    rcol_r,
    pt,
    ft,
    load_sem,
    a_send,
    a_recv,
    b_send,
    b_recv,
    cf_send,
    cf_recv,
    halo_send,
    halo_recv,
    ok_halo,
    ok_rim,
):
    t = lax.axis_index("tile")
    s = lax.axis_index("slab")
    t_prev, t_next = lax.rem(t + nt - 1, nt), lax.rem(t + 1, nt)
    s_prev, s_next = lax.rem(s + ns - 1, ns), lax.rem(s + 1, ns)
    n_y = ns // 4
    y, core = lax.rem(lax.div(s, 2), n_y), lax.rem(s, 2)
    g = lax.div(s, 2 * n_y) * 2 + core

    def slab_at(gg, yy):
        return lax.div(gg, 2) * (2 * n_y) + yy * 2 + lax.rem(gg, 2)

    def place(j):
        return j // 2 % n_y, j // (2 * n_y) * 2 + j % 2

    others_g = [lax.rem(g + d, 4) for d in range(1, 4)]
    others_y = [lax.rem(y + d, n_y) for d in range(1, n_y)]

    half = nt // 2
    late_up, early_up = (t > 0) & (t != half), t == half
    late_down, early_down = t == half - 1, (t < nt - 1) & (t != half - 1)

    inside = pl.ds(1, nz)
    loads = []
    for i, (src, dst) in enumerate(
        [
            (v_h, v_s.at[inside]),
            (s_h, s_s.at[inside]),
            (k_h, k_s),
            (al_h, al_s),
            (pond_h, pond),
            (sx_h, sx),
            (sy_h, sy),
            (man_h, man),
            (riv_h, riv),
            (code_h, code),
            (ph_h, ph_s),
        ]
    ):
        copy = pltpu.make_async_copy(src, dst, load_sem.at[i])
        copy.start()
        loads.append(copy)

    barrier = pltpu.get_barrier_semaphore()

    def greet(tt, ss):
        pl.semaphore_signal(barrier, inc=1, device_id=(tt, ss), device_id_type=MESH)

    for gg in others_g:
        greet(t, slab_at(gg, y))
    for yy in others_y:
        greet(t, slab_at(g, yy))
    greet(t, jnp.where(core == 1, s_next, s_prev))

    def greet_tile(mine, other, s_in, s_late):
        @pl.when(mine)
        def _():
            greet(other, s)

            @pl.when(s == s_in)
            def _():
                greet(other, s_late)

    greet_tile(early_down, t_next, ns - 1, 0)
    greet_tile(early_up, t_prev, 0, ns - 1)

    zero = jnp.zeros((H, W), jnp.float32)
    for ref in (v_s, s_s, sa, sb):
        ref[0] = zero
        ref[nz + 1] = zero

    fields = ((v_s, 1), (s_s, 1), (k_s, 0), (al_s, 0))
    for f, (ref, first) in enumerate(fields):
        loads[f].wait()
        for layer in range(nz):
            k = f * nz + layer
            row_up[k : k + 1, :] = ref[layer + first, 0:1, :]
            row_dn[k : k + 1, :] = ref[layer + first, H - 1 : H, :]

    for j in range(ns):
        lo, hi = max(R * j - 1, 0), min(R * j + R + 1, H)
        at = lo - (R * j - 1)
        yj, gj = place(j)
        top_stage[gj, yj, at : at + hi - lo, :] = v_s[1, lo:hi, :]
    top_stage[0, 0, 0:1, :] = v_s[1, 0:1, :]
    top_stage[3, n_y - 1, R + 1 : R + 2, :] = v_s[1, H - 1 : H, :]

    late = late_up.astype(jnp.int32), late_down.astype(jnp.int32)
    at_first, at_last = (s == 0).astype(jnp.int32), (s == ns - 1).astype(jnp.int32)
    pl.semaphore_wait(
        barrier,
        3 + n_y + late[0] * (1 + at_first) + late[1] * (1 + at_last),
    )

    def send(src, dst, send_sem, recv_sem, tt, ss):
        return pltpu.make_async_remote_copy(
            src_ref=src,
            dst_ref=dst,
            send_sem=send_sem,
            recv_sem=recv_sem,
            device_id=(tt, ss),
            device_id_type=MESH,
        )

    row_copies = [
        send(row_up, rrow_dn, halo_send.at[0], halo_recv.at[0], t_prev, s),
        send(row_dn, rrow_up, halo_send.at[1], halo_recv.at[1], t_next, s),
    ]
    tile_flows = [
        send(cm_stage, rcm, cf_send.at[1], cf_recv.at[1], t_prev, ns - 1),
        send(cp_stage, rcp, cf_send.at[0], cf_recv.at[0], t_next, 0),
    ]
    slab_coefs = [
        send(cm_stage, rcm, cf_send.at[1], cf_recv.at[1], t, s_prev),
        send(cp_stage, rcp, cf_send.at[0], cf_recv.at[0], t, s_next),
    ]
    col_copies = [
        send(col_l, rcol_r, halo_send.at[2], halo_recv.at[2], t, s_prev),
        send(col_r, rcol_l, halo_send.at[3], halo_recv.at[3], t, s_next),
    ]

    first_stage = [
        send(top_stage.at[gg], mid.at[g], a_send.at[d], a_recv.at[g], t, slab_at(gg, y))
        for d, gg in enumerate(others_g)
    ]
    first_arrivals = [
        send(top_stage.at[gg], mid.at[gg], a_send.at[d], a_recv.at[gg], t, slab_at(gg, y))
        for d, gg in enumerate(others_g)
    ]
    second_stage = [
        send(mid.at[:, yy], rtop.at[y], b_send.at[d], b_recv.at[y], t, slab_at(g, yy))
        for d, yy in enumerate(others_y)
    ]
    second_arrivals = [
        send(mid.at[:, yy], rtop.at[yy], b_send.at[d], b_recv.at[yy], t, slab_at(g, yy))
        for d, yy in enumerate(others_y)
    ]

    def late_sends(mine, side, other, s_late):
        @pl.when(mine)
        def _():
            row_copies[side].start()
            pl.semaphore_signal(
                ok_halo.at[1 - side], inc=1, device_id=(other, s), device_id_type=MESH
            )

            @pl.when(s == s_late)
            def _():
                pl.semaphore_signal(
                    ok_rim.at[1 - side],
                    inc=1,
                    device_id=(other, ns - 1 - s_late),
                    device_id_type=MESH,
                )

    late_sends(late_down, 1, t_next, ns - 1)
    late_sends(late_up, 0, t_prev, 0)

    for copy in first_stage:
        copy.start()
    mid[g] = top_stage[g]

    for i in range(4, 10):
        loads[i].wait()
    for j in range(ns):
        cols = slice(j * W, j * W + W)
        conveyance = (5.0 / 3.0) * jnp.exp((2.0 / 3.0) * jnp.log(pond[:, cols])) / man[:, cols]
        along, beside = sx[:, cols], sy[:, cols]
        cx = jnp.where(riv[:, cols] == 1, 0.0, conveyance * (along * lax.rsqrt(along)))
        cy = conveyance * (beside * lax.rsqrt(beside))
        bits = code[:, cols]
        xp = jnp.where((bits & 1) == 1, cx, 0.0)
        xm = cx - xp
        yp = jnp.where(lax.shift_right_logical(bits, 1) == 1, cy, 0.0)
        c_all[j] = cx + cy
        c_xp[j, 0:1, :] = jnp.zeros((1, W), jnp.float32)
        c_xp[j, 1:R, :] = xp[0 : R - 1]
        c_xm[j, 0 : R - 1, :] = xm[1:R]
        c_xm[j, R - 1 : R, :] = jnp.zeros((1, W), jnp.float32)
        c_yp[j] = yp
        c_ym[j] = cy - yp
        cp_stage[j] = xp[R - 1 : R]
        cm_stage[j] = xm[0:1]

    @pl.when(s > 0)
    def _():
        slab_coefs[0].start()

    @pl.when(s < ns - 1)
    def _():
        slab_coefs[1].start()

    lane = lax.broadcasted_iota(jnp.int32, (8, W), 1)
    sub = lax.broadcasted_iota(jnp.int32, (8, W), 0)
    pair = lax.shift_right_logical(lane, 1)
    edges = [jnp.zeros((8, W), jnp.float32) for _ in range(H // 8)]
    for f, (ref, first) in enumerate(fields):
        for layer in range(nz):
            k = f * nz + layer
            here = pair == k
            for c in range(H // 8):
                x = ref[layer + first, c * 8 : c * 8 + 8, :]
                edges[c] = jnp.where(here, pltpu.roll(x, 2 * k + 1, 1), edges[c])
    pt[...] = jnp.concatenate(edges, axis=0).T
    col_l[...] = pt[pl.ds(1, 4 * nz, stride=2), :]
    col_r[...] = pt[pl.ds(0, 4 * nz, stride=2), :]
    for copy in col_copies:
        copy.start()

    loads[10].wait()
    inner_lane = lane < W - 1
    first_row = sub == 0

    def one_layer(layer):
        lp = layer + 1
        before = jnp.maximum(layer - 1, 0)
        for c in range(H // 8):
            rows = slice(c * 8, c * 8 + 8)
            v = v_s[lp, rows, :]
            a, b, sat_deriv, saturation = half_state(
                v, s_s[lp, rows, :], k_s[layer, rows, :], al_s[layer, rows, :]
            )
            sa[lp, rows, :] = a
            sb[lp, rows, :] = b
            out[layer, rows, :] = (
                specific_storage * saturation + ph_s[layer, rows, :] * sat_deriv
            ) * v
        carried = jnp.zeros((8, W), jnp.float32)
        for c in range(H // 8):
            rows = slice(c * 8, c * 8 + 8)
            here = [ref[lp, rows, :] for ref in (v_s, s_s, sa, sb)]
            beside = [pltpu.roll(x, W - 1, 1) for x in here]
            flux = jnp.where(inner_lane, face(*here, *beside), 0.0)
            total = out[layer, rows, :] + flux - pltpu.roll(flux, 1, 1)
            if c < H // 8 - 1:
                after = slice(c * 8 + 1, c * 8 + 9)
                flux = face(*here, *[ref[lp, after, :] for ref in (v_s, s_s, sa, sb)])
            else:
                flux = jnp.where(sub == 7, 0.0, face(*here, *[pltpu.roll(x, 7, 0) for x in here]))
            shifted = pltpu.roll(flux, 1, 0)
            total = total + flux - jnp.where(first_row, carried, shifted)
            carried = shifted
            v, suction, a, b = here
            above = [ref[layer, rows, :] for ref in (v_s, s_s, sa, sb)]
            flux = (a + above[2]) * (above[0] - v) + (b + above[3]) * (suction - above[1] + 1.0)
            out[before, rows, :] = out[before, rows, :] + flux
            out[layer, rows, :] = total - flux

    pl.loop(0, nz // 2)(one_layer)
    for copy in first_arrivals:
        copy.wait_recv()
    for copy in second_stage:
        copy.start()
    rtop[y] = mid[:, y]
    pl.loop(nz // 2, nz)(one_layer)

    for c in range(H // 8):
        rows = slice(c * 8, c * 8 + 8)
        out[nz - 1, rows, :] = (
            out[nz - 1, rows, :]
            + sa[nz, rows, :] * v_s[nz, rows, :]
            + sb[nz, rows, :] * (1.0 - s_s[nz, rows, :])
        )

    def parts(ref):
        return [ref[f * nz : f * nz + nz, :] for f in range(4)]

    def edge_state(raw):
        a, b, _, _ = half_state(*raw)
        return raw[0], raw[1], a, b

    def outside(exists, raw):
        return [jnp.where(exists, x, 0.0) for x in edge_state(raw)]

    def early_rows(mine, side):
        @pl.when(mine)
        def _():
            pl.semaphore_wait(ok_halo.at[side], 1)
            row_copies[side].start()

    def early_flow(mine, side):
        @pl.when(mine)
        def _():
            pl.semaphore_wait(ok_rim.at[side], 1)
            tile_flows[side].start()

    early_rows(early_down, 1)

    for copy in col_copies:
        copy.wait_recv()
    ft[...] = jnp.zeros(ft.shape, jnp.float32)
    ft[pl.ds(1, nz, stride=2), :] = face(
        *edge_state(parts(col_l)), *outside(s > 0, parts(rcol_l))
    )
    ft[pl.ds(0, nz, stride=2), :] = face(
        *edge_state(parts(col_r)), *outside(s < ns - 1, parts(rcol_r))
    )
    turned = ft[...].T
    rim_lane = (lane == 0) | (lane == W - 1)
    for layer in range(nz):
        for c in range(H // 8):
            rows = slice(c * 8, c * 8 + 8)
            x = pltpu.roll(turned[rows], W - (2 * layer + 1), 1)
            out[layer, rows, :] = out[layer, rows, :] + jnp.where(rim_lane, x, 0.0)

    @pl.when(s > 0)
    def _():
        slab_coefs[1].wait_recv()
        for j in range(ns):
            c_xp[j, 0:1, :] = rcp[j]

    @pl.when(s < ns - 1)
    def _():
        slab_coefs[0].wait_recv()
        for j in range(ns):
            c_xm[j, R - 1 : R, :] = rcm[j]

    for copy in second_arrivals:
        copy.wait_recv()

    def top_rows(j, rows):
        yj, gj = place(j)
        return rtop[yj, gj, rows, :]

    @pl.when((s == 0) & (t > 0))
    def _():
        for j in range(ns):
            cm_stage[j] = cm_stage[j] * top_rows(j, slice(1, 2))

    @pl.when((s == ns - 1) & (t < nt - 1))
    def _():
        for j in range(ns):
            cp_stage[j] = cp_stage[j] * top_rows(j, slice(R, R + 1))

    @pl.when(late_up & (s == 0))
    def _():
        tile_flows[0].start()

    @pl.when(late_down & (s == ns - 1))
    def _():
        tile_flows[1].start()

    early_flow(early_down & (s == ns - 1), 1)

    small_lane = lax.broadcasted_iota(jnp.int32, (R, W), 1)
    first, last = small_lane == 0, small_lane == W - 1
    nil = jnp.zeros((R, W), jnp.float32)
    prev_plus = nil
    tops = [top_rows(j, slice(1, R + 1)) for j in range(ns)]
    minus = [pltpu.roll(c_ym[j] * tops[j], W - 1, 1) for j in range(ns)] + [nil]
    for j in range(ns):
        plus = pltpu.roll(c_yp[j] * tops[j], 1, 1)
        surf[:, j * W : j * W + W] = (
            c_all[j] * tops[j]
            - c_xp[j] * top_rows(j, slice(0, R))
            - c_xm[j] * top_rows(j, slice(2, R + 2))
            - jnp.where(first, prev_plus, plus)
            - jnp.where(last, minus[j + 1], minus[j])
        )
        prev_plus = plus

    early_rows(early_up, 0)
    early_flow(early_up & (s == 0), 0)

    def add_rows(exists, copy, own, theirs, row):
        @pl.when(exists)
        def _():
            copy.wait_recv()
            flux = face(*edge_state(parts(own)), *edge_state(parts(theirs)))
            for layer in range(nz):
                out[layer, row : row + 1, :] = (
                    out[layer, row : row + 1, :] + flux[layer : layer + 1]
                )

        @pl.when(jnp.logical_not(exists))
        def _():
            v, suction, a, b = edge_state(parts(own))
            flux = a * v - b * suction
            for layer in range(nz):
                out[layer, row : row + 1, :] = (
                    out[layer, row : row + 1, :] + flux[layer : layer + 1]
                )

    add_rows(t < nt - 1, row_copies[0], row_dn, rrow_dn, H - 1)
    add_rows(t > 0, row_copies[1], row_up, rrow_up, 0)

    def add_flow(exists, copy, arrived, row):
        @pl.when(exists)
        def _():
            copy.wait_recv()
            for j in range(ns):
                cols = slice(j * W, j * W + W)
                surf[row : row + 1, cols] = surf[row : row + 1, cols] - arrived[j]

    add_flow((t < nt - 1) & (s == ns - 1), tile_flows[0], rcm, R - 1)
    add_flow((t > 0) & (s == 0), tile_flows[1], rcp, 0)

    for copy in col_copies:
        copy.wait_send()
    for side, exists in ((0, t > 0), (1, t < nt - 1)):

        @pl.when(exists)
        def _(side=side):
            row_copies[side].wait_send()

    @pl.when((s > 0) | (t > 0))
    def _():
        slab_coefs[0].wait_send()

    @pl.when((s < ns - 1) | (t < nt - 1))
    def _():
        slab_coefs[1].wait_send()

    for copy in first_stage + second_stage:
        copy.wait_send()


def per_device(nt, ns, *args):
    nz, H, _ = args[0].shape
    R = args[5].shape[0]
    f32 = jnp.float32
    vm = pltpu.VMEM
    dma = pltpu.SemaphoreType.DMA
    anywhere = pl.BlockSpec(memory_space=pl.ANY)
    return pl.pallas_call(
        functools.partial(kernel, nt, ns, nz, H, R),
        out_shape=(
            vm((nz, H, W), f32),
            vm((R, ns * W), f32),
        ),
        in_specs=[anywhere] * 11,
        out_specs=(pl.BlockSpec(memory_space=pltpu.VMEM),) * 2,
        scratch_shapes=[
            vm((nz + 2, H, W), f32),
            vm((nz + 2, H, W), f32),
            vm((nz, H, W), f32),
            vm((nz, H, W), f32),
            vm((nz, H, W), f32),
            vm((nz + 2, H, W), f32),
            vm((nz + 2, H, W), f32),
            vm((R, ns * W), f32),
            vm((R, ns * W), f32),
            vm((R, ns * W), f32),
            vm((R, ns * W), f32),
            vm((R, ns * W), jnp.int32),
            vm((R, ns * W), jnp.int32),
            vm((ns, R, W), f32),
            vm((ns, R, W), f32),
            vm((ns, R, W), f32),
            vm((ns, R, W), f32),
            vm((ns, R, W), f32),
            vm((4, ns // 4, R + 2, W), f32),
            vm((4, ns // 4, R + 2, W), f32),
            vm((ns // 4, 4, R + 2, W), f32),
            vm((ns, 1, W), f32),
            vm((ns, 1, W), f32),
            vm((ns, 1, W), f32),
            vm((ns, 1, W), f32),
            vm((4 * nz, W), f32),
            vm((4 * nz, W), f32),
            vm((4 * nz, W), f32),
            vm((4 * nz, W), f32),
            vm((4 * nz, H), f32),
            vm((4 * nz, H), f32),
            vm((4 * nz, H), f32),
            vm((4 * nz, H), f32),
            vm((W, H), f32),
            vm((W, H), f32),
            dma((11,)),
            dma((4,)),
            dma((4,)),
            dma((ns // 4,)),
            dma((ns // 4,)),
            dma((2,)),
            dma((2,)),
            dma((4,)),
            dma((4,)),
            pltpu.SemaphoreType.REGULAR((2,)),
            pltpu.SemaphoreType.REGULAR((2,)),
        ],
        compiler_params=pltpu.CompilerParams(
            collective_id=0, has_side_effects=True, vmem_limit_bytes=56 * 1024 * 1024
        ),
    )(*args)


def solution(mesh):
    cells = P(None, "tile", "slab")
    surface = P(("tile", "slab"), None)
    return jax.shard_map(
        functools.partial(per_device, mesh.shape["tile"], mesh.shape["slab"]),
        mesh=mesh,
        in_specs=(cells,) * 5 + (surface,) * 6,
        out_specs=(cells, surface),
        check_vma=False,
    )
```

```python
import functools

import jax
import jax.numpy as jnp
from jax import lax
from jax.experimental import pallas as pl
from jax.experimental.pallas import tpu as pltpu
from jax.sharding import PartitionSpec as P

MESH = pl.DeviceIdType.MESH
W = 128
specific_storage = 0.01


def relative(suction, vg_alpha):
    w = vg_alpha * suction
    saturation = lax.rsqrt(1.0 + w * w)
    quarter = saturation * lax.rsqrt(saturation)
    bracket = 1.0 - w * saturation
    return w, saturation, quarter, bracket


def half_state(v, suction, conductivity, vg_alpha):
    w, saturation, quarter, bracket = relative(suction, vg_alpha)
    kb = conductivity * quarter * bracket
    m = vg_alpha * saturation * saturation
    a = 0.5 * kb * bracket
    b = kb * m * (0.25 * bracket * w + saturation) * v
    return a, b, w * m * saturation, saturation


def face(v, s, a, b, vj, sj, aj, bj):
    return (a + aj) * (v - vj) + (b + bj) * (sj - s)


def kernel(
    nt,
    ns,
    nz,
    H,
    R,
    v_h,
    s_h,
    k_h,
    al_h,
    ph_h,
    pond_h,
    sx_h,
    sy_h,
    man_h,
    riv_h,
    code_h,
    out,
    surf,
    v_s,
    s_s,
    k_s,
    al_s,
    ph_s,
    sa,
    sb,
    pond,
    sx,
    sy,
    man,
    riv,
    code,
    c_all,
    c_xp,
    c_xm,
    c_yp,
    c_ym,
    top_stage,
    rtop,
    rim_stage,
    rim,
    cp_stage,
    cm_stage,
    rcp,
    rcm,
    row_up,
    row_dn,
    rrow_up,
    rrow_dn,
    col_l,
    col_r,
    rcol_l,
    rcol_r,
    pt,
    ft,
    load_sem,
    top_send,
    top_recv,
    rim_send,
    rim_recv,
    cf_send,
    cf_recv,
    halo_send,
    halo_recv,
    ok_halo,
    ok_rim,
):
    t = lax.axis_index("tile")
    s = lax.axis_index("slab")
    t_prev, t_next = lax.rem(t + nt - 1, nt), lax.rem(t + 1, nt)
    s_prev, s_next = lax.rem(s + ns - 1, ns), lax.rem(s + 1, ns)
    half = nt // 2
    early_up = (t == half) | (t == 1)
    late_up = (t > 0) & jnp.logical_not(early_up)
    late_down = (t == half - 1) | (t == 0)
    early_down = (t < nt - 1) & jnp.logical_not(late_down)

    inside = pl.ds(1, nz)
    loads = []
    for i, (src, dst) in enumerate(
        [
            (v_h, v_s.at[inside]),
            (s_h, s_s.at[inside]),
            (k_h, k_s),
            (al_h, al_s),
            (pond_h, pond),
            (sx_h, sx),
            (sy_h, sy),
            (man_h, man),
            (riv_h, riv),
            (code_h, code),
            (ph_h, ph_s),
        ]
    ):
        copy = pltpu.make_async_copy(src, dst, load_sem.at[i])
        loads.append(copy)
    loads[0].start()

    barrier = pltpu.get_barrier_semaphore()

    def greet(tt, ss):
        pl.semaphore_signal(barrier, inc=1, device_id=(tt, ss), device_id_type=MESH)

    for d in range(ns // 2):
        for peer in {ns // 2 - d, ns // 2 + d} - {ns}:
            greet(t, lax.rem(s + peer, ns))

    def greet_tile(mine, other, s_in):
        @pl.when(mine)
        def _():
            @pl.when(s == s_in)
            def _():
                @pl.loop(0, ns)
                def _(j):
                    greet(other, j)

            @pl.when(s != s_in)
            def _():
                greet(other, s)

    greet_tile(early_down, t_next, ns - 1)
    greet_tile(early_up, t_prev, 0)
    for copy in loads[1:]:
        copy.start()

    loads[0].wait()
    rim_stage[0] = v_s[1, 0:1, :]
    rim_stage[1] = v_s[1, H - 1 : H, :]
    for j in range(ns):
        lo, hi = max(R * j - 1, 0), min(R * j + R + 1, H)
        at = lo - (R * j - 1)
        top_stage[j, at : at + hi - lo, :] = v_s[1, lo:hi, :]
    top_stage[0, 0:1, :] = v_s[1, 0:1, :]
    top_stage[ns - 1, R + 1 : R + 2, :] = v_s[1, H - 1 : H, :]

    fields = ((v_s, 1), (s_s, 1), (k_s, 0), (al_s, 0))

    lane = lax.broadcasted_iota(jnp.int32, (8, W), 1)
    sub = lax.broadcasted_iota(jnp.int32, (8, W), 0)
    pair = lax.shift_right_logical(lane, 1)

    def local_rows():
        zero = jnp.zeros((H, W), jnp.float32)
        for ref in (v_s, s_s, sa, sb):
            ref[0] = zero
            ref[nz + 1] = zero

        for f, (ref, first) in enumerate(fields):
            if f > 0:
                loads[f].wait()
            for layer in range(nz):
                k = f * nz + layer
                row_up[k : k + 1, :] = ref[layer + first, 0:1, :]
                row_dn[k : k + 1, :] = ref[layer + first, H - 1 : H, :]

    def local_coefficients():
        for i in range(4, 10):
            loads[i].wait()
        for j in range(ns):
            cols = slice(j * W, j * W + W)
            conveyance = (5.0 / 3.0) * jnp.exp((2.0 / 3.0) * jnp.log(pond[:, cols])) / man[:, cols]
            along, beside = sx[:, cols], sy[:, cols]
            cx = jnp.where(riv[:, cols] == 1, 0.0, conveyance * (along * lax.rsqrt(along)))
            cy = conveyance * (beside * lax.rsqrt(beside))
            bits = code[:, cols]
            xp = jnp.where((bits & 1) == 1, cx, 0.0)
            xm = cx - xp
            yp = jnp.where(lax.shift_right_logical(bits, 1) == 1, cy, 0.0)
            c_all[j] = cx + cy
            c_xp[j, 0:1, :] = jnp.zeros((1, W), jnp.float32)
            c_xp[j, 1:R, :] = xp[0 : R - 1]
            c_xm[j, 0 : R - 1, :] = xm[1:R]
            c_xm[j, R - 1 : R, :] = jnp.zeros((1, W), jnp.float32)
            c_yp[j] = yp
            c_ym[j] = cy - yp
            cp_stage[j : j + 1, :] = xp[R - 1 : R]
            cm_stage[j : j + 1, :] = xm[0:1]

    def local_columns():
        edges = [jnp.zeros((8, W), jnp.float32) for _ in range(H // 8)]
        for f, (ref, first) in enumerate(fields):
            for layer in range(nz):
                k = f * nz + layer
                here = pair == k
                for c in range(H // 8):
                    x = ref[layer + first, c * 8 : c * 8 + 8, :]
                    edges[c] = jnp.where(here, pltpu.roll(x, 2 * k + 1, 1), edges[c])
        pt[...] = jnp.concatenate(edges, axis=0).T
        col_l[...] = pt[pl.ds(1, 4 * nz, stride=2), :]
        col_r[...] = pt[pl.ds(0, 4 * nz, stride=2), :]
        loads[10].wait()

    inner_lane = lane < W - 1
    first_row = sub == 0

    def one_layer(layer):
        lp = layer + 1
        before = jnp.maximum(layer - 1, 0)
        for c in range(H // 8):
            rows = slice(c * 8, c * 8 + 8)
            v = v_s[lp, rows, :]
            a, b, sat_deriv, saturation = half_state(
                v, s_s[lp, rows, :], k_s[layer, rows, :], al_s[layer, rows, :]
            )
            sa[lp, rows, :] = a
            sb[lp, rows, :] = b
            out[layer, rows, :] = (
                specific_storage * saturation + ph_s[layer, rows, :] * sat_deriv
            ) * v
        carried = jnp.zeros((8, W), jnp.float32)
        for c in range(H // 8):
            rows = slice(c * 8, c * 8 + 8)
            here = [ref[lp, rows, :] for ref in (v_s, s_s, sa, sb)]
            beside = [pltpu.roll(x, W - 1, 1) for x in here]
            flux = jnp.where(inner_lane, face(*here, *beside), 0.0)
            total = out[layer, rows, :] + flux - pltpu.roll(flux, 1, 1)
            if c < H // 8 - 1:
                after = slice(c * 8 + 1, c * 8 + 9)
                flux = face(*here, *[ref[lp, after, :] for ref in (v_s, s_s, sa, sb)])
            else:
                flux = jnp.where(sub == 7, 0.0, face(*here, *[pltpu.roll(x, 7, 0) for x in here]))
            shifted = pltpu.roll(flux, 1, 0)
            total = total + flux - jnp.where(first_row, carried, shifted)
            carried = shifted
            v, suction, a, b = here
            above = [ref[layer, rows, :] for ref in (v_s, s_s, sa, sb)]
            flux = (a + above[2]) * (above[0] - v) + (b + above[3]) * (suction - above[1] + 1.0)
            out[before, rows, :] = out[before, rows, :] + flux
            out[layer, rows, :] = total - flux

    patient = (t == 0) & (s > 0)
    prepared = (t == 0) | (t == half - 1)
    pl.when(prepared)(local_rows)
    pl.when(prepared)(local_coefficients)
    pl.when(patient)(local_columns)
    pl.loop(0, jnp.where(patient, nz, 0))(one_layer)

    late = late_up.astype(jnp.int32), late_down.astype(jnp.int32)
    at_first, at_last = (s == 0).astype(jnp.int32), (s == ns - 1).astype(jnp.int32)
    pl.semaphore_wait(
        barrier,
        ns - 1 + late[0] * (2 - at_last) + late[1] * (2 - at_first),
    )

    def send(src, dst, send_sem, recv_sem, tt, ss):
        return pltpu.make_async_remote_copy(
            src_ref=src,
            dst_ref=dst,
            send_sem=send_sem,
            recv_sem=recv_sem,
            device_id=(tt, ss),
            device_id_type=MESH,
        )

    row_copies = [
        send(row_up, rrow_dn, halo_send.at[0], halo_recv.at[0], t_prev, s),
        send(row_dn, rrow_up, halo_send.at[1], halo_recv.at[1], t_next, s),
    ]
    rims = [
        send(rim_stage.at[0], rim.at[s], rim_send.at[0], rim_recv.at[0], t_prev, ns - 1),
        send(rim_stage.at[1], rim.at[s], rim_send.at[1], rim_recv.at[0], t_next, 0),
    ]
    tile_flows = [
        send(cm_stage, rcm, cf_send.at[1], cf_recv.at[1], t_prev, ns - 1),
        send(cp_stage, rcp, cf_send.at[0], cf_recv.at[0], t_next, 0),
    ]
    slab_coefs = [
        send(cm_stage, rcm, cf_send.at[1], cf_recv.at[1], t, s_prev),
        send(cp_stage, rcp, cf_send.at[0], cf_recv.at[0], t, s_next),
    ]
    col_copies = [
        send(col_l, rcol_r, halo_send.at[2], halo_recv.at[2], t, s_prev),
        send(col_r, rcol_l, halo_send.at[3], halo_recv.at[3], t, s_next),
    ]

    peers = [lax.rem(s + d, ns) for d in range(1, ns)]
    tops = [
        send(top_stage.at[peer], rtop.at[s], top_send.at[0], top_recv.at[0], t, peer)
        for peer in peers
    ]
    all_tops = send(
        top_stage.at[1:], rtop.at[1:], top_send.at[0], top_recv.at[0], t, s_next
    )
    all_rims = send(rim, rim, rim_send.at[0], rim_recv.at[0], t_next, 0)

    def late_sends(mine, side, other, s_late):
        @pl.when(mine)
        def _():
            row_copies[side].start()
            pl.semaphore_signal(
                ok_halo.at[1 - side], inc=1, device_id=(other, s), device_id_type=MESH
            )

            @pl.when(s == s_late)
            def _():
                pl.semaphore_signal(
                    ok_rim.at[1 - side],
                    inc=1,
                    device_id=(other, ns - 1 - s_late),
                    device_id_type=MESH,
                )

    for side, exists in ((1, late_down), (0, late_up)):
        pl.when(exists)(rims[side].start)

    @pl.when(late_down & (s == ns - 1))
    def _():
        tile_flows[1].start()

    late_sends(late_down, 1, t_next, ns - 1)
    for copy in tops:
        copy.start()
    rtop[s] = top_stage[s]
    unprepared = jnp.logical_not(prepared)
    pl.when(unprepared)(local_rows)
    late_sends(late_up, 0, t_prev, 0)
    pl.when(unprepared)(local_coefficients)

    @pl.when(late_up & (s == 0))
    def _():
        tile_flows[0].start()

    pl.when(jnp.logical_not(patient))(local_columns)


    @pl.when(s > 0)
    def _():
        slab_coefs[0].start()

    @pl.when(s < ns - 1)
    def _():
        slab_coefs[1].start()

    for copy in col_copies:
        copy.start()

    def early_rows(mine, side):
        @pl.when(mine)
        def _():
            pl.semaphore_wait(ok_halo.at[side], 1)
            row_copies[side].start()

    def early_flow(mine, side):
        @pl.when(mine)
        def _():
            pl.semaphore_wait(ok_rim.at[side], 1)
            tile_flows[side].start()

    def top_rows(j, rows):
        return rtop[j, rows, :]

    flowing = early_down & (s == ns - 1)
    middle = jnp.where(flowing, nz // 2, nz)
    pl.loop(jnp.where(patient, nz, 0), middle)(one_layer)

    @pl.when(flowing)
    def _():
        all_tops.wait_recv()
        for j in range(ns):
            cp_stage[j : j + 1, :] = cp_stage[j : j + 1, :] * top_rows(j, slice(R, R + 1))

    early_flow(flowing, 1)
    pl.loop(middle, nz)(one_layer)

    for c in range(H // 8):
        rows = slice(c * 8, c * 8 + 8)
        out[nz - 1, rows, :] = (
            out[nz - 1, rows, :]
            + sa[nz, rows, :] * v_s[nz, rows, :]
            + sb[nz, rows, :] * (1.0 - s_s[nz, rows, :])
        )

    def parts(ref):
        return [ref[f * nz : f * nz + nz, :] for f in range(4)]

    def edge_state(raw):
        a, b, _, _ = half_state(*raw)
        return raw[0], raw[1], a, b

    def outside(exists, raw):
        return [jnp.where(exists, x, 0.0) for x in edge_state(raw)]

    early_rows(early_down, 1)
    if half != 1:
        early_rows(t == 1, 0)

    pl.when(jnp.logical_not(flowing))(all_tops.wait_recv)

    @pl.when(early_up & (s == 0))
    def _():
        for j in range(ns):
            cm_stage[j : j + 1, :] = cm_stage[j : j + 1, :] * top_rows(j, slice(1, 2))

    for copy in col_copies:
        copy.wait_recv()
    ft[...] = jnp.zeros(ft.shape, jnp.float32)
    ft[pl.ds(1, nz, stride=2), :] = face(
        *edge_state(parts(col_l)), *outside(s > 0, parts(rcol_l))
    )
    ft[pl.ds(0, nz, stride=2), :] = face(
        *edge_state(parts(col_r)), *outside(s < ns - 1, parts(rcol_r))
    )
    turned = ft[...].T
    rim_lane = (lane == 0) | (lane == W - 1)
    for layer in range(nz):
        for c in range(H // 8):
            rows = slice(c * 8, c * 8 + 8)
            x = pltpu.roll(turned[rows], W - (2 * layer + 1), 1)
            out[layer, rows, :] = out[layer, rows, :] + jnp.where(rim_lane, x, 0.0)

    @pl.when(s > 0)
    def _():
        slab_coefs[1].wait_recv()
        for j in range(ns):
            c_xp[j, 0:1, :] = rcp[j : j + 1, :]

    @pl.when(s < ns - 1)
    def _():
        slab_coefs[0].wait_recv()
        for j in range(ns):
            c_xm[j, R - 1 : R, :] = rcm[j : j + 1, :]

    small_lane = lax.broadcasted_iota(jnp.int32, (R, W), 1)
    first, last = small_lane == 0, small_lane == W - 1
    nil = jnp.zeros((R, W), jnp.float32)
    prev_plus = nil
    own = [top_rows(j, slice(1, R + 1)) for j in range(ns)]
    minus = [pltpu.roll(c_ym[j] * own[j], W - 1, 1) for j in range(ns)] + [nil]
    for j in range(ns):
        plus = pltpu.roll(c_yp[j] * own[j], 1, 1)
        surf[:, j * W : j * W + W] = (
            c_all[j] * own[j]
            - c_xp[j] * top_rows(j, slice(0, R))
            - c_xm[j] * top_rows(j, slice(2, R + 2))
            - jnp.where(first, prev_plus, plus)
            - jnp.where(last, minus[j + 1], minus[j])
        )
        prev_plus = plus

    early_rows(t == half, 0)
    early_flow(early_up & (s == 0), 0)

    def add_rows(exists, copy, own, theirs, row):
        @pl.when(exists)
        def _():
            copy.wait_recv()
            flux = face(*edge_state(parts(own)), *edge_state(parts(theirs)))
            for layer in range(nz):
                out[layer, row : row + 1, :] = (
                    out[layer, row : row + 1, :] + flux[layer : layer + 1]
                )

        @pl.when(jnp.logical_not(exists))
        def _():
            v, suction, a, b = edge_state(parts(own))
            flux = a * v - b * suction
            for layer in range(nz):
                out[layer, row : row + 1, :] = (
                    out[layer, row : row + 1, :] + flux[layer : layer + 1]
                )

    add_rows(t < nt - 1, row_copies[0], row_dn, rrow_dn, H - 1)
    add_rows(t > 0, row_copies[1], row_up, rrow_up, 0)

    def add_flow(early, late, copy, arrived, row):
        @pl.when(late)
        def _():
            copy.wait_recv()
            for j in range(ns):
                cols = slice(j * W, j * W + W)
                surf[row : row + 1, cols] = surf[row : row + 1, cols] - arrived[j : j + 1, :]

        @pl.when(early)
        def _():
            copy.wait_recv()

            all_rims.wait_recv()
            for j in range(ns):
                cols = slice(j * W, j * W + W)
                surf[row : row + 1, cols] = surf[row : row + 1, cols] - arrived[j : j + 1, :] * rim[j]

    at_end, at_start = s == ns - 1, s == 0
    add_flow(early_down & at_end, late_down & at_end, tile_flows[0], rcm, R - 1)
    add_flow(early_up & at_start, late_up & at_start, tile_flows[1], rcp, 0)

    for copy in col_copies:
        copy.wait_send()
    for side, exists in ((0, t > 0), (1, t < nt - 1)):

        @pl.when(exists)
        def _(side=side):
            row_copies[side].wait_send()

    for side, exists in ((0, late_up), (1, late_down)):

        @pl.when(exists)
        def _(side=side):
            rims[side].wait_send()

    @pl.when((s > 0) | (t > 0))
    def _():
        slab_coefs[0].wait_send()

    @pl.when((s < ns - 1) | (t < nt - 1))
    def _():
        slab_coefs[1].wait_send()

    all_tops.wait_send()


def per_device(nt, ns, *args):
    nz, H, _ = args[0].shape
    R = args[5].shape[0]
    f32 = jnp.float32
    vm = pltpu.VMEM
    dma = pltpu.SemaphoreType.DMA
    anywhere = pl.BlockSpec(memory_space=pl.ANY)
    return pl.pallas_call(
        functools.partial(kernel, nt, ns, nz, H, R),
        out_shape=(
            vm((nz, H, W), f32),
            vm((R, ns * W), f32),
        ),
        in_specs=[anywhere] * 11,
        out_specs=(pl.BlockSpec(memory_space=pltpu.VMEM),) * 2,
        scratch_shapes=[
            vm((nz + 2, H, W), f32),
            vm((nz + 2, H, W), f32),
            vm((nz, H, W), f32),
            vm((nz, H, W), f32),
            vm((nz, H, W), f32),
            vm((nz + 2, H, W), f32),
            vm((nz + 2, H, W), f32),
            vm((R, ns * W), f32),
            vm((R, ns * W), f32),
            vm((R, ns * W), f32),
            vm((R, ns * W), f32),
            vm((R, ns * W), jnp.int32),
            vm((R, ns * W), jnp.int32),
            vm((ns, R, W), f32),
            vm((ns, R, W), f32),
            vm((ns, R, W), f32),
            vm((ns, R, W), f32),
            vm((ns, R, W), f32),
            vm((ns, R + 2, W), f32),
            vm((ns, R + 2, W), f32),
            vm((2, 1, W), f32),
            vm((ns, 1, W), f32),
            vm((ns, W), f32),
            vm((ns, W), f32),
            vm((ns, W), f32),
            vm((ns, W), f32),
            vm((4 * nz, W), f32),
            vm((4 * nz, W), f32),
            vm((4 * nz, W), f32),
            vm((4 * nz, W), f32),
            vm((4 * nz, H), f32),
            vm((4 * nz, H), f32),
            vm((4 * nz, H), f32),
            vm((4 * nz, H), f32),
            vm((W, H), f32),
            vm((W, H), f32),
            dma((11,)),
            dma((1,)),
            dma((1,)),
            dma((2,)),
            dma((1,)),
            dma((2,)),
            dma((2,)),
            dma((4,)),
            dma((4,)),
            pltpu.SemaphoreType.REGULAR((2,)),
            pltpu.SemaphoreType.REGULAR((2,)),
        ],
        compiler_params=pltpu.CompilerParams(
            collective_id=0, has_side_effects=True, vmem_limit_bytes=56 * 1024 * 1024
        ),
    )(*args)


def solution(mesh):
    cells = P(None, "tile", "slab")
    surface = P(("tile", "slab"), None)
    return jax.shard_map(
        functools.partial(per_device, mesh.shape["tile"], mesh.shape["slab"]),
        mesh=mesh,
        in_specs=(cells,) * 5 + (surface,) * 6,
        out_specs=(cells, surface),
        check_vma=False,
    )
```

```python
import functools

import jax
import jax.numpy as jnp
from jax import lax
from jax.experimental import pallas as pl
from jax.experimental.pallas import tpu as pltpu
from jax.sharding import PartitionSpec as P

MESH = pl.DeviceIdType.MESH
W = 128
specific_storage = 0.01


def relative(suction, vg_alpha):
    w = vg_alpha * suction
    saturation = lax.rsqrt(1.0 + w * w)
    quarter = saturation * lax.rsqrt(saturation)
    bracket = 1.0 - w * saturation
    return w, saturation, quarter, bracket


def half_state(v, suction, conductivity, vg_alpha):
    w, saturation, quarter, bracket = relative(suction, vg_alpha)
    kb = conductivity * quarter * bracket
    m = vg_alpha * saturation * saturation
    a = 0.5 * kb * bracket
    b = kb * m * (0.25 * bracket * w + saturation) * v
    return a, b, w * m * saturation, saturation


def face(v, s, a, b, vj, sj, aj, bj):
    return (a + aj) * (v - vj) + (b + bj) * (sj - s)


def kernel(
    nt,
    ns,
    nz,
    H,
    R,
    v_h,
    s_h,
    k_h,
    al_h,
    ph_h,
    pond_h,
    sx_h,
    sy_h,
    man_h,
    riv_h,
    code_h,
    out,
    surf,
    v_s,
    s_s,
    k_s,
    al_s,
    ph_s,
    sa,
    sb,
    pond,
    sx,
    sy,
    man,
    riv,
    code,
    c_all,
    c_xp,
    c_xm,
    c_yp,
    c_ym,
    top_stage,
    rtop,
    rim_stage,
    rim,
    cp_stage,
    cm_stage,
    rcp,
    rcm,
    row_up,
    row_dn,
    rrow_up,
    rrow_dn,
    col_l,
    col_r,
    rcol_l,
    rcol_r,
    pt,
    ft,
    load_sem,
    top_send,
    top_recv,
    rim_send,
    rim_recv,
    cf_send,
    cf_recv,
    halo_send,
    halo_recv,
    ok_halo,
    ok_rim,
    ok_slab,
):
    t = lax.axis_index("tile")
    s = lax.axis_index("slab")
    t_prev, t_next = lax.rem(t + nt - 1, nt), lax.rem(t + 1, nt)
    s_prev, s_next = lax.rem(s + ns - 1, ns), lax.rem(s + 1, ns)
    half = nt // 2
    early_up = (t == half) | (t == 1) | ((t == half - 1) & (t > 0))
    late_up = (t > 0) & jnp.logical_not(early_up)
    late_down = (t == half - 1) | (t == half - 2) | (t == 0)
    early_down = (t < nt - 1) & jnp.logical_not(late_down)

    inside = pl.ds(1, nz)
    loads = []
    for i, (src, dst) in enumerate(
        [
            (v_h, v_s.at[inside]),
            (s_h, s_s.at[inside]),
            (k_h, k_s),
            (al_h, al_s),
            (pond_h, pond),
            (sx_h, sx),
            (sy_h, sy),
            (man_h, man),
            (riv_h, riv),
            (code_h, code),
            (ph_h, ph_s),
        ]
    ):
        copy = pltpu.make_async_copy(src, dst, load_sem.at[i])
        loads.append(copy)
    loads[0].start()

    barrier = pltpu.get_barrier_semaphore()

    def greet(tt, ss):
        pl.semaphore_signal(barrier, inc=1, device_id=(tt, ss), device_id_type=MESH)

    n_y = ns // 4
    ranked = t == half - 1
    n_below = jnp.where(ranked, s, ns - 1)

    def is_above(peer):
        return ranked & (peer > s)

    def wrapped(peer):
        return jnp.where(peer >= ns, peer - ns, peer)

    @pl.loop(s + 1, jnp.where(ranked, ns, s + ns))
    def _(peer):
        greet(t, wrapped(peer))

    def greet_tile(mine, other, s_in):
        @pl.when(mine)
        def _():
            @pl.when(s == s_in)
            def _():
                @pl.loop(0, ns)
                def _(j):
                    greet(other, j)

            @pl.when(s != s_in)
            def _():
                greet(other, s)

    greet_tile(early_down, t_next, ns - 1)
    greet_tile(early_up, t_prev, 0)
    for copy in loads[1:]:
        copy.start()

    loads[0].wait()
    rim_stage[0] = v_s[1, 0:1, :]
    rim_stage[1] = v_s[1, H - 1 : H, :]
    for j in range(ns):
        lo, hi = max(R * j - 1, 0), min(R * j + R + 1, H)
        at = lo - (R * j - 1)
        top_stage[j, at : at + hi - lo, :] = v_s[1, lo:hi, :]
    top_stage[0, 0:1, :] = v_s[1, 0:1, :]
    top_stage[ns - 1, R + 1 : R + 2, :] = v_s[1, H - 1 : H, :]

    fields = ((v_s, 1), (s_s, 1), (k_s, 0), (al_s, 0))

    lane = lax.broadcasted_iota(jnp.int32, (8, W), 1)
    sub = lax.broadcasted_iota(jnp.int32, (8, W), 0)
    pair = lax.shift_right_logical(lane, 1)

    def local_rows():
        zero = jnp.zeros((H, W), jnp.float32)
        for ref in (v_s, s_s, sa, sb):
            ref[0] = zero
            ref[nz + 1] = zero

        for f, (ref, first) in enumerate(fields):
            if f > 0:
                loads[f].wait()
            for layer in range(nz):
                k = f * nz + layer
                row_up[k : k + 1, :] = ref[layer + first, 0:1, :]
                row_dn[k : k + 1, :] = ref[layer + first, H - 1 : H, :]

    def local_coefficients():
        for i in range(4, 10):
            loads[i].wait()
        for j in range(ns):
            cols = slice(j * W, j * W + W)
            conveyance = (5.0 / 3.0) * jnp.exp((2.0 / 3.0) * jnp.log(pond[:, cols])) / man[:, cols]
            along, beside = sx[:, cols], sy[:, cols]
            cx = jnp.where(riv[:, cols] == 1, 0.0, conveyance * (along * lax.rsqrt(along)))
            cy = conveyance * (beside * lax.rsqrt(beside))
            bits = code[:, cols]
            xp = jnp.where((bits & 1) == 1, cx, 0.0)
            xm = cx - xp
            yp = jnp.where(lax.shift_right_logical(bits, 1) == 1, cy, 0.0)
            c_all[j] = cx + cy
            c_xp[j, 0:1, :] = jnp.zeros((1, W), jnp.float32)
            c_xp[j, 1:R, :] = xp[0 : R - 1]
            c_xm[j, 0 : R - 1, :] = xm[1:R]
            c_xm[j, R - 1 : R, :] = jnp.zeros((1, W), jnp.float32)
            c_yp[j] = yp
            c_ym[j] = cy - yp
            cp_stage[j : j + 1, :] = xp[R - 1 : R]
            cm_stage[j : j + 1, :] = xm[0:1]

    def local_columns():
        edges = [jnp.zeros((8, W), jnp.float32) for _ in range(H // 8)]
        for f, (ref, first) in enumerate(fields):
            for layer in range(nz):
                k = f * nz + layer
                here = pair == k
                for c in range(H // 8):
                    x = ref[layer + first, c * 8 : c * 8 + 8, :]
                    edges[c] = jnp.where(here, pltpu.roll(x, 2 * k + 1, 1), edges[c])
        pt[...] = jnp.concatenate(edges, axis=0).T
        col_l[...] = pt[pl.ds(1, 4 * nz, stride=2), :]
        col_r[...] = pt[pl.ds(0, 4 * nz, stride=2), :]
        loads[10].wait()

    inner_lane = lane < W - 1
    first_row = sub == 0

    def one_layer(layer):
        lp = layer + 1
        before = jnp.maximum(layer - 1, 0)
        for c in range(H // 8):
            rows = slice(c * 8, c * 8 + 8)
            v = v_s[lp, rows, :]
            a, b, sat_deriv, saturation = half_state(
                v, s_s[lp, rows, :], k_s[layer, rows, :], al_s[layer, rows, :]
            )
            sa[lp, rows, :] = a
            sb[lp, rows, :] = b
            out[layer, rows, :] = (
                specific_storage * saturation + ph_s[layer, rows, :] * sat_deriv
            ) * v
        carried = jnp.zeros((8, W), jnp.float32)
        for c in range(H // 8):
            rows = slice(c * 8, c * 8 + 8)
            here = [ref[lp, rows, :] for ref in (v_s, s_s, sa, sb)]
            beside = [pltpu.roll(x, W - 1, 1) for x in here]
            flux = jnp.where(inner_lane, face(*here, *beside), 0.0)
            total = out[layer, rows, :] + flux - pltpu.roll(flux, 1, 1)
            if c < H // 8 - 1:
                after = slice(c * 8 + 1, c * 8 + 9)
                flux = face(*here, *[ref[lp, after, :] for ref in (v_s, s_s, sa, sb)])
            else:
                flux = jnp.where(sub == 7, 0.0, face(*here, *[pltpu.roll(x, 7, 0) for x in here]))
            shifted = pltpu.roll(flux, 1, 0)
            total = total + flux - jnp.where(first_row, carried, shifted)
            carried = shifted
            v, suction, a, b = here
            above = [ref[layer, rows, :] for ref in (v_s, s_s, sa, sb)]
            flux = (a + above[2]) * (above[0] - v) + (b + above[3]) * (suction - above[1] + 1.0)
            out[before, rows, :] = out[before, rows, :] + flux
            out[layer, rows, :] = total - flux

    patient = (t == 0) & (s > 0)
    y = lax.rem(lax.div(s, 2), n_y)
    last_started = (s >= ns // 2) & (y >= n_y // 2 - 1) & (y < n_y - 2)
    prepared = patient | ((t == half - 1) & (s > 0) & jnp.logical_not(last_started))
    prepared = prepared | (late_down & (s == ns - 1))
    pl.when(prepared)(local_rows)
    pl.when(prepared)(local_coefficients)
    pl.when(patient)(local_columns)
    pl.loop(0, jnp.where(patient, nz, 0))(one_layer)

    late = late_up.astype(jnp.int32), late_down.astype(jnp.int32)
    at_first, at_last = (s == 0).astype(jnp.int32), (s == ns - 1).astype(jnp.int32)
    pl.semaphore_wait(
        barrier,
        n_below + late[0] * (2 - at_last) + late[1] * (2 - at_first),
    )

    def send(src, dst, send_sem, recv_sem, tt, ss):
        return pltpu.make_async_remote_copy(
            src_ref=src,
            dst_ref=dst,
            send_sem=send_sem,
            recv_sem=recv_sem,
            device_id=(tt, ss),
            device_id_type=MESH,
        )

    row_copies = [
        send(row_up, rrow_dn, halo_send.at[0], halo_recv.at[0], t_prev, s),
        send(row_dn, rrow_up, halo_send.at[1], halo_recv.at[1], t_next, s),
    ]
    rims = [
        send(rim_stage.at[0], rim.at[s], rim_send.at[0], rim_recv.at[0], t_prev, ns - 1),
        send(rim_stage.at[1], rim.at[s], rim_send.at[1], rim_recv.at[0], t_next, 0),
    ]
    tile_flows = [
        send(cm_stage, rcm, cf_send.at[1], cf_recv.at[1], t_prev, ns - 1),
        send(cp_stage, rcp, cf_send.at[0], cf_recv.at[0], t_next, 0),
    ]
    slab_coefs = [
        send(cm_stage, rcm, cf_send.at[1], cf_recv.at[1], t, s_prev),
        send(cp_stage, rcp, cf_send.at[0], cf_recv.at[0], t, s_next),
    ]
    col_copies = [
        send(col_l, rcol_r, halo_send.at[2], halo_recv.at[2], t, s_prev),
        send(col_r, rcol_l, halo_send.at[3], halo_recv.at[3], t, s_next),
    ]

    def top_copy(peer):
        return send(
            top_stage.at[peer], rtop.at[s], top_send.at[0], top_recv.at[0], t, peer
        )

    all_tops = send(
        top_stage.at[1:], rtop.at[1:], top_send.at[0], top_recv.at[0], t, s_next
    )
    all_rims = send(rim, rim, rim_send.at[0], rim_recv.at[0], t_next, 0)

    def late_sends(mine, side, other, s_late):
        @pl.when(mine)
        def _():
            row_copies[side].start()
            pl.semaphore_signal(
                ok_halo.at[1 - side], inc=1, device_id=(other, s), device_id_type=MESH
            )

            @pl.when(s == s_late)
            def _():
                pl.semaphore_signal(
                    ok_rim.at[1 - side],
                    inc=1,
                    device_id=(other, ns - 1 - s_late),
                    device_id_type=MESH,
                )

    for side, exists in ((1, late_down), (0, late_up)):
        pl.when(exists)(rims[side].start)

    @pl.when(late_down & (s == ns - 1))
    def _():
        tile_flows[1].start()

    late_sends(late_down & prepared, 1, t_next, ns - 1)

    @pl.loop(jnp.where(ranked, 0, s + 1), jnp.where(ranked, s, s + ns))
    def _(peer):
        top_copy(wrapped(peer)).start()

    @pl.loop(0, jnp.where(ranked, s, 0))
    def _(peer):
        pl.semaphore_signal(ok_slab, inc=1, device_id=(t, peer), device_id_type=MESH)

    rtop[s] = top_stage[s]
    unprepared = jnp.logical_not(prepared)
    pl.when(unprepared)(local_rows)
    late_sends(late_down & unprepared, 1, t_next, ns - 1)
    late_sends(late_up, 0, t_prev, 0)
    pl.when(unprepared)(local_coefficients)

    @pl.when(late_up & (s == 0))
    def _():
        tile_flows[0].start()

    pl.when(jnp.logical_not(patient))(local_columns)


    near = [
        (slab_coefs[0], s_prev, s > 0),
        (slab_coefs[1], s_next, s < ns - 1),
        (col_copies[0], s_prev, s >= 0),
        (col_copies[1], s_next, s >= 0),
    ]
    for copy, peer, exists in near:
        pl.when(exists & jnp.logical_not(is_above(peer)))(copy.start)

    def early_rows(mine, side):
        @pl.when(mine)
        def _():
            pl.semaphore_wait(ok_halo.at[side], 1)
            row_copies[side].start()

    def early_flow(mine, side):
        @pl.when(mine)
        def _():
            pl.semaphore_wait(ok_rim.at[side], 1)
            tile_flows[side].start()

    def top_rows(j, rows):
        return rtop[j, rows, :]

    flowing = early_down & (s == ns - 1)
    middle = jnp.where(flowing | ranked, nz // 2, nz)
    pl.loop(jnp.where(patient, nz, 0), middle)(one_layer)

    @pl.when(ranked)
    def _():
        @pl.when(n_below < ns - 1)
        def _():
            pl.semaphore_wait(ok_slab, ns - 1 - n_below)

        @pl.loop(s + 1, ns)
        def _(peer):
            top_copy(peer).start()

        for copy, peer, exists in near:
            pl.when(exists & is_above(peer))(copy.start)

    @pl.when(flowing)
    def _():
        all_tops.wait_recv()
        for j in range(ns):
            cp_stage[j : j + 1, :] = cp_stage[j : j + 1, :] * top_rows(j, slice(R, R + 1))

    early_flow(flowing, 1)
    pl.loop(jnp.where(patient, nz, middle), nz)(one_layer)

    for c in range(H // 8):
        rows = slice(c * 8, c * 8 + 8)
        out[nz - 1, rows, :] = (
            out[nz - 1, rows, :]
            + sa[nz, rows, :] * v_s[nz, rows, :]
            + sb[nz, rows, :] * (1.0 - s_s[nz, rows, :])
        )

    def parts(ref):
        return [ref[f * nz : f * nz + nz, :] for f in range(4)]

    def edge_state(raw):
        a, b, _, _ = half_state(*raw)
        return raw[0], raw[1], a, b

    def outside(exists, raw):
        return [jnp.where(exists, x, 0.0) for x in edge_state(raw)]

    early_rows(early_down, 1)
    if half != 1:
        early_rows((t == 1) | (t == half - 1), 0)

    for copy in col_copies:
        copy.wait_recv()
    ft[...] = jnp.zeros(ft.shape, jnp.float32)
    ft[pl.ds(1, nz, stride=2), :] = face(
        *edge_state(parts(col_l)), *outside(s > 0, parts(rcol_l))
    )
    ft[pl.ds(0, nz, stride=2), :] = face(
        *edge_state(parts(col_r)), *outside(s < ns - 1, parts(rcol_r))
    )
    turned = ft[...].T
    rim_lane = (lane == 0) | (lane == W - 1)
    for layer in range(nz):
        for c in range(H // 8):
            rows = slice(c * 8, c * 8 + 8)
            x = pltpu.roll(turned[rows], W - (2 * layer + 1), 1)
            out[layer, rows, :] = out[layer, rows, :] + jnp.where(rim_lane, x, 0.0)

    pl.when(jnp.logical_not(flowing))(all_tops.wait_recv)

    @pl.when(early_up & (s == 0))
    def _():
        for j in range(ns):
            cm_stage[j : j + 1, :] = cm_stage[j : j + 1, :] * top_rows(j, slice(1, 2))

    @pl.when(s > 0)
    def _():
        slab_coefs[1].wait_recv()
        for j in range(ns):
            c_xp[j, 0:1, :] = rcp[j : j + 1, :]

    @pl.when(s < ns - 1)
    def _():
        slab_coefs[0].wait_recv()
        for j in range(ns):
            c_xm[j, R - 1 : R, :] = rcm[j : j + 1, :]

    small_lane = lax.broadcasted_iota(jnp.int32, (R, W), 1)
    first, last = small_lane == 0, small_lane == W - 1
    nil = jnp.zeros((R, W), jnp.float32)
    prev_plus = nil
    own = [top_rows(j, slice(1, R + 1)) for j in range(ns)]
    minus = [pltpu.roll(c_ym[j] * own[j], W - 1, 1) for j in range(ns)] + [nil]
    for j in range(ns):
        plus = pltpu.roll(c_yp[j] * own[j], 1, 1)
        surf[:, j * W : j * W + W] = (
            c_all[j] * own[j]
            - c_xp[j] * top_rows(j, slice(0, R))
            - c_xm[j] * top_rows(j, slice(2, R + 2))
            - jnp.where(first, prev_plus, plus)
            - jnp.where(last, minus[j + 1], minus[j])
        )
        prev_plus = plus

    early_rows(t == half, 0)
    early_flow(early_up & (s == 0), 0)

    def add_rows(exists, copy, own, theirs, row):
        @pl.when(exists)
        def _():
            copy.wait_recv()
            flux = face(*edge_state(parts(own)), *edge_state(parts(theirs)))
            for layer in range(nz):
                out[layer, row : row + 1, :] = (
                    out[layer, row : row + 1, :] + flux[layer : layer + 1]
                )

        @pl.when(jnp.logical_not(exists))
        def _():
            v, suction, a, b = edge_state(parts(own))
            flux = a * v - b * suction
            for layer in range(nz):
                out[layer, row : row + 1, :] = (
                    out[layer, row : row + 1, :] + flux[layer : layer + 1]
                )

    add_rows(t < nt - 1, row_copies[0], row_dn, rrow_dn, H - 1)
    add_rows(t > 0, row_copies[1], row_up, rrow_up, 0)

    def add_flow(early, late, copy, arrived, row):
        @pl.when(late)
        def _():
            copy.wait_recv()
            for j in range(ns):
                cols = slice(j * W, j * W + W)
                surf[row : row + 1, cols] = surf[row : row + 1, cols] - arrived[j : j + 1, :]

        @pl.when(early)
        def _():
            copy.wait_recv()

            all_rims.wait_recv()
            for j in range(ns):
                cols = slice(j * W, j * W + W)
                surf[row : row + 1, cols] = surf[row : row + 1, cols] - arrived[j : j + 1, :] * rim[j]

    at_end, at_start = s == ns - 1, s == 0
    add_flow(early_down & at_end, late_down & at_end, tile_flows[0], rcm, R - 1)
    add_flow(early_up & at_start, late_up & at_start, tile_flows[1], rcp, 0)

    for copy in col_copies:
        copy.wait_send()
    for side, exists in ((0, t > 0), (1, t < nt - 1)):

        @pl.when(exists)
        def _(side=side):
            row_copies[side].wait_send()

    for side, exists in ((0, late_up), (1, late_down)):

        @pl.when(exists)
        def _(side=side):
            rims[side].wait_send()

    @pl.when((s > 0) | (t > 0))
    def _():
        slab_coefs[0].wait_send()

    @pl.when((s < ns - 1) | (t < nt - 1))
    def _():
        slab_coefs[1].wait_send()

    all_tops.wait_send()


def per_device(nt, ns, *args):
    nz, H, _ = args[0].shape
    R = args[5].shape[0]
    f32 = jnp.float32
    vm = pltpu.VMEM
    dma = pltpu.SemaphoreType.DMA
    anywhere = pl.BlockSpec(memory_space=pl.ANY)
    return pl.pallas_call(
        functools.partial(kernel, nt, ns, nz, H, R),
        out_shape=(
            vm((nz, H, W), f32),
            vm((R, ns * W), f32),
        ),
        in_specs=[anywhere] * 11,
        out_specs=(pl.BlockSpec(memory_space=pltpu.VMEM),) * 2,
        scratch_shapes=[
            vm((nz + 2, H, W), f32),
            vm((nz + 2, H, W), f32),
            vm((nz, H, W), f32),
            vm((nz, H, W), f32),
            vm((nz, H, W), f32),
            vm((nz + 2, H, W), f32),
            vm((nz + 2, H, W), f32),
            vm((R, ns * W), f32),
            vm((R, ns * W), f32),
            vm((R, ns * W), f32),
            vm((R, ns * W), f32),
            vm((R, ns * W), jnp.int32),
            vm((R, ns * W), jnp.int32),
            vm((ns, R, W), f32),
            vm((ns, R, W), f32),
            vm((ns, R, W), f32),
            vm((ns, R, W), f32),
            vm((ns, R, W), f32),
            vm((ns, R + 2, W), f32),
            vm((ns, R + 2, W), f32),
            vm((2, 1, W), f32),
            vm((ns, 1, W), f32),
            vm((ns, W), f32),
            vm((ns, W), f32),
            vm((ns, W), f32),
            vm((ns, W), f32),
            vm((4 * nz, W), f32),
            vm((4 * nz, W), f32),
            vm((4 * nz, W), f32),
            vm((4 * nz, W), f32),
            vm((4 * nz, H), f32),
            vm((4 * nz, H), f32),
            vm((4 * nz, H), f32),
            vm((4 * nz, H), f32),
            vm((W, H), f32),
            vm((W, H), f32),
            dma((11,)),
            dma((1,)),
            dma((1,)),
            dma((2,)),
            dma((1,)),
            dma((2,)),
            dma((2,)),
            dma((4,)),
            dma((4,)),
            pltpu.SemaphoreType.REGULAR((2,)),
            pltpu.SemaphoreType.REGULAR((2,)),
            pltpu.SemaphoreType.REGULAR,
        ],
        compiler_params=pltpu.CompilerParams(
            collective_id=0, has_side_effects=True, vmem_limit_bytes=56 * 1024 * 1024
        ),
    )(*args)


def solution(mesh):
    cells = P(None, "tile", "slab")
    surface = P(("tile", "slab"), None)
    return jax.shard_map(
        functools.partial(per_device, mesh.shape["tile"], mesh.shape["slab"]),
        mesh=mesh,
        in_specs=(cells,) * 5 + (surface,) * 6,
        out_specs=(cells, surface),
        check_vma=False,
    )
```

```python
import functools

import jax
import jax.numpy as jnp
from jax import lax
from jax.experimental import pallas as pl
from jax.experimental.pallas import tpu as pltpu
from jax.sharding import PartitionSpec as P

MESH = pl.DeviceIdType.MESH
W = 128
specific_storage = 0.01


def relative(suction, vg_alpha):
    w = vg_alpha * suction
    saturation = lax.rsqrt(1.0 + w * w)
    quarter = saturation * lax.rsqrt(saturation)
    bracket = 1.0 - w * saturation
    return w, saturation, quarter, bracket


def half_state(v, suction, conductivity, vg_alpha):
    w, saturation, quarter, bracket = relative(suction, vg_alpha)
    kb = conductivity * quarter * bracket
    m = vg_alpha * saturation * saturation
    a = 0.5 * kb * bracket
    b = kb * m * (0.25 * bracket * w + saturation) * v
    return a, b, w * m * saturation, saturation


def face(v, s, a, b, vj, sj, aj, bj):
    return (a + aj) * (v - vj) + (b + bj) * (sj - s)


def kernel(
    nt,
    ns,
    nz,
    H,
    R,
    v_h,
    s_h,
    k_h,
    al_h,
    ph_h,
    pond_h,
    sx_h,
    sy_h,
    man_h,
    riv_h,
    code_h,
    out,
    surf,
    v_s,
    s_s,
    k_s,
    al_s,
    ph_s,
    sa,
    sb,
    pond,
    sx,
    sy,
    man,
    riv,
    code,
    c_all,
    c_xp,
    c_xm,
    c_yp,
    c_ym,
    top_stage,
    rtop,
    rim_stage,
    rim,
    cp_stage,
    cm_stage,
    rcp,
    rcm,
    row_up,
    row_dn,
    rrow_up,
    rrow_dn,
    col_l,
    col_r,
    rcol_l,
    rcol_r,
    pt,
    ft,
    load_sem,
    top_send,
    top_recv,
    rim_send,
    rim_recv,
    cf_send,
    cf_recv,
    halo_send,
    halo_recv,
    ok_halo,
    ok_rim,
    ok_slab,
):
    t = lax.axis_index("tile")
    s = lax.axis_index("slab")
    t_prev, t_next = lax.rem(t + nt - 1, nt), lax.rem(t + 1, nt)
    s_prev, s_next = lax.rem(s + ns - 1, ns), lax.rem(s + 1, ns)
    half = nt // 2
    early_up = (t == half) | (t == 1) | ((t == half - 1) & (t > 0))
    late_up = (t > 0) & jnp.logical_not(early_up)
    late_down = (t == half - 1) | (t == half - 2) | (t == 0)
    early_down = (t < nt - 1) & jnp.logical_not(late_down)

    inside = pl.ds(1, nz)
    loads = []
    for i, (src, dst) in enumerate(
        [
            (v_h, v_s.at[inside]),
            (s_h, s_s.at[inside]),
            (k_h, k_s),
            (al_h, al_s),
            (pond_h, pond),
            (sx_h, sx),
            (sy_h, sy),
            (man_h, man),
            (riv_h, riv),
            (code_h, code),
            (ph_h, ph_s),
        ]
    ):
        copy = pltpu.make_async_copy(src, dst, load_sem.at[i])
        loads.append(copy)
    loads[0].start()

    barrier = pltpu.get_barrier_semaphore()

    def greet(tt, ss):
        pl.semaphore_signal(barrier, inc=1, device_id=(tt, ss), device_id_type=MESH)

    ranked = t == half - 1
    n_below = jnp.where(ranked, s, ns - 1)

    def is_above(peer):
        return ranked & (peer > s)

    def wrapped(peer):
        return jnp.where(peer >= ns, peer - ns, peer)

    @pl.loop(s + 1, jnp.where(ranked, ns, s + ns))
    def _(peer):
        greet(t, wrapped(peer))

    def greet_tile(mine, other, s_in):
        @pl.when(mine)
        def _():
            @pl.when(s == s_in)
            def _():
                @pl.loop(0, ns)
                def _(j):
                    greet(other, j)

            @pl.when(s != s_in)
            def _():
                greet(other, s)

    greet_tile(early_down, t_next, ns - 1)
    greet_tile(early_up, t_prev, 0)
    for copy in loads[1:]:
        copy.start()

    loads[0].wait()
    rim_stage[0] = v_s[1, 0:1, :]
    rim_stage[1] = v_s[1, H - 1 : H, :]
    for j in range(ns):
        lo, hi = max(R * j - 1, 0), min(R * j + R + 1, H)
        at = lo - (R * j - 1)
        top_stage[j, at : at + hi - lo, :] = v_s[1, lo:hi, :]
    top_stage[0, 0:1, :] = v_s[1, 0:1, :]
    top_stage[ns - 1, R + 1 : R + 2, :] = v_s[1, H - 1 : H, :]

    fields = ((v_s, 1), (s_s, 1), (k_s, 0), (al_s, 0))

    lane = lax.broadcasted_iota(jnp.int32, (8, W), 1)
    sub = lax.broadcasted_iota(jnp.int32, (8, W), 0)
    pair = lax.shift_right_logical(lane, 1)

    def local_rows():
        zero = jnp.zeros((H, W), jnp.float32)
        for ref in (v_s, s_s, sa, sb):
            ref[0] = zero
            ref[nz + 1] = zero

        for f, (ref, first) in enumerate(fields):
            if f > 0:
                loads[f].wait()
            for layer in range(nz):
                k = f * nz + layer
                row_up[k : k + 1, :] = ref[layer + first, 0:1, :]
                row_dn[k : k + 1, :] = ref[layer + first, H - 1 : H, :]

    def local_coefficients():
        for i in range(4, 10):
            loads[i].wait()
        for j in range(ns):
            cols = slice(j * W, j * W + W)
            conveyance = (5.0 / 3.0) * jnp.exp((2.0 / 3.0) * jnp.log(pond[:, cols])) / man[:, cols]
            along, beside = sx[:, cols], sy[:, cols]
            cx = jnp.where(riv[:, cols] == 1, 0.0, conveyance * (along * lax.rsqrt(along)))
            cy = conveyance * (beside * lax.rsqrt(beside))
            bits = code[:, cols]
            xp = jnp.where((bits & 1) == 1, cx, 0.0)
            xm = cx - xp
            yp = jnp.where(lax.shift_right_logical(bits, 1) == 1, cy, 0.0)
            c_all[j] = cx + cy
            c_xp[j, 0:1, :] = jnp.zeros((1, W), jnp.float32)
            c_xp[j, 1:R, :] = xp[0 : R - 1]
            c_xm[j, 0 : R - 1, :] = xm[1:R]
            c_xm[j, R - 1 : R, :] = jnp.zeros((1, W), jnp.float32)
            c_yp[j] = yp
            c_ym[j] = cy - yp
            cp_stage[j : j + 1, :] = xp[R - 1 : R]
            cm_stage[j : j + 1, :] = xm[0:1]

    def local_columns():
        edges = [jnp.zeros((8, W), jnp.float32) for _ in range(H // 8)]
        for f, (ref, first) in enumerate(fields):
            for layer in range(nz):
                k = f * nz + layer
                here = pair == k
                for c in range(H // 8):
                    x = ref[layer + first, c * 8 : c * 8 + 8, :]
                    edges[c] = jnp.where(here, pltpu.roll(x, 2 * k + 1, 1), edges[c])
        pt[...] = jnp.concatenate(edges, axis=0).T
        col_l[...] = pt[pl.ds(1, 4 * nz, stride=2), :]
        col_r[...] = pt[pl.ds(0, 4 * nz, stride=2), :]
        loads[10].wait()

    inner_lane = lane < W - 1
    first_row = sub == 0

    def one_layer(layer):
        lp = layer + 1
        before = jnp.maximum(layer - 1, 0)
        for c in range(H // 8):
            rows = slice(c * 8, c * 8 + 8)
            v = v_s[lp, rows, :]
            a, b, sat_deriv, saturation = half_state(
                v, s_s[lp, rows, :], k_s[layer, rows, :], al_s[layer, rows, :]
            )
            sa[lp, rows, :] = a
            sb[lp, rows, :] = b
            out[layer, rows, :] = (
                specific_storage * saturation + ph_s[layer, rows, :] * sat_deriv
            ) * v
        carried = jnp.zeros((8, W), jnp.float32)
        for c in range(H // 8):
            rows = slice(c * 8, c * 8 + 8)
            here = [ref[lp, rows, :] for ref in (v_s, s_s, sa, sb)]
            beside = [pltpu.roll(x, W - 1, 1) for x in here]
            flux = jnp.where(inner_lane, face(*here, *beside), 0.0)
            total = out[layer, rows, :] + flux - pltpu.roll(flux, 1, 1)
            if c < H // 8 - 1:
                after = slice(c * 8 + 1, c * 8 + 9)
                flux = face(*here, *[ref[lp, after, :] for ref in (v_s, s_s, sa, sb)])
            else:
                flux = jnp.where(sub == 7, 0.0, face(*here, *[pltpu.roll(x, 7, 0) for x in here]))
            shifted = pltpu.roll(flux, 1, 0)
            total = total + flux - jnp.where(first_row, carried, shifted)
            carried = shifted
            v, suction, a, b = here
            above = [ref[layer, rows, :] for ref in (v_s, s_s, sa, sb)]
            flux = (a + above[2]) * (above[0] - v) + (b + above[3]) * (suction - above[1] + 1.0)
            out[before, rows, :] = out[before, rows, :] + flux
            out[layer, rows, :] = total - flux

    patient = (t == 0) & (s > 0)
    prepared = patient | (late_down & (s == ns - 1))
    pl.when(prepared)(local_rows)
    pl.when(prepared)(local_coefficients)
    pl.when(patient)(local_columns)
    pl.loop(0, jnp.where(patient, nz, 0))(one_layer)

    late = late_up.astype(jnp.int32), late_down.astype(jnp.int32)
    at_first, at_last = (s == 0).astype(jnp.int32), (s == ns - 1).astype(jnp.int32)
    pl.semaphore_wait(
        barrier,
        n_below + late[0] * (2 - at_last) + late[1] * (2 - at_first),
    )

    def send(src, dst, send_sem, recv_sem, tt, ss):
        return pltpu.make_async_remote_copy(
            src_ref=src,
            dst_ref=dst,
            send_sem=send_sem,
            recv_sem=recv_sem,
            device_id=(tt, ss),
            device_id_type=MESH,
        )

    row_copies = [
        send(row_up, rrow_dn, halo_send.at[0], halo_recv.at[0], t_prev, s),
        send(row_dn, rrow_up, halo_send.at[1], halo_recv.at[1], t_next, s),
    ]
    rims = [
        send(rim_stage.at[0], rim.at[s], rim_send.at[0], rim_recv.at[0], t_prev, ns - 1),
        send(rim_stage.at[1], rim.at[s], rim_send.at[1], rim_recv.at[0], t_next, 0),
    ]
    tile_flows = [
        send(cm_stage, rcm, cf_send.at[1], cf_recv.at[1], t_prev, ns - 1),
        send(cp_stage, rcp, cf_send.at[0], cf_recv.at[0], t_next, 0),
    ]
    slab_coefs = [
        send(cm_stage, rcm, cf_send.at[1], cf_recv.at[1], t, s_prev),
        send(cp_stage, rcp, cf_send.at[0], cf_recv.at[0], t, s_next),
    ]
    col_copies = [
        send(col_l, rcol_r, halo_send.at[2], halo_recv.at[2], t, s_prev),
        send(col_r, rcol_l, halo_send.at[3], halo_recv.at[3], t, s_next),
    ]

    def top_copy(peer):
        return send(
            top_stage.at[peer], rtop.at[s], top_send.at[0], top_recv.at[0], t, peer
        )

    all_tops = send(
        top_stage.at[1:], rtop.at[1:], top_send.at[0], top_recv.at[0], t, s_next
    )
    all_rims = send(rim, rim, rim_send.at[0], rim_recv.at[0], t_next, 0)

    def late_sends(mine, side, other, s_late):
        @pl.when(mine)
        def _():
            row_copies[side].start()
            pl.semaphore_signal(
                ok_halo.at[1 - side], inc=1, device_id=(other, s), device_id_type=MESH
            )

            @pl.when(s == s_late)
            def _():
                pl.semaphore_signal(
                    ok_rim.at[1 - side],
                    inc=1,
                    device_id=(other, ns - 1 - s_late),
                    device_id_type=MESH,
                )

    for side, exists in ((1, late_down), (0, late_up)):
        pl.when(exists)(rims[side].start)

    @pl.when(late_down & (s == ns - 1))
    def _():
        tile_flows[1].start()

    late_sends(late_down & prepared, 1, t_next, ns - 1)

    @pl.loop(jnp.where(ranked, 0, s + 1), jnp.where(ranked, s, s + ns))
    def _(peer):
        top_copy(wrapped(peer)).start()

    @pl.loop(0, jnp.where(ranked, s, 0))
    def _(peer):
        pl.semaphore_signal(ok_slab, inc=1, device_id=(t, peer), device_id_type=MESH)

    rtop[s] = top_stage[s]
    unprepared = jnp.logical_not(prepared)
    pl.when(unprepared)(local_rows)
    late_sends(late_down & unprepared, 1, t_next, ns - 1)
    late_sends(late_up, 0, t_prev, 0)
    pl.when(unprepared)(local_coefficients)

    @pl.when(late_up & (s == 0))
    def _():
        tile_flows[0].start()

    pl.when(jnp.logical_not(patient))(local_columns)


    near = [
        (slab_coefs[0], s_prev, s > 0),
        (slab_coefs[1], s_next, s < ns - 1),
        (col_copies[0], s_prev, s >= 0),
        (col_copies[1], s_next, s >= 0),
    ]
    for copy, peer, exists in near:
        pl.when(exists & jnp.logical_not(is_above(peer)))(copy.start)

    def early_rows(mine, side):
        @pl.when(mine)
        def _():
            pl.semaphore_wait(ok_halo.at[side], 1)
            row_copies[side].start()

    def early_flow(mine, side):
        @pl.when(mine)
        def _():
            pl.semaphore_wait(ok_rim.at[side], 1)
            tile_flows[side].start()

    def top_rows(j, rows):
        return rtop[j, rows, :]

    flowing = early_down & (s == ns - 1)
    middle = jnp.where(flowing | ranked, nz // 2, nz)
    pl.loop(jnp.where(patient, nz, 0), middle)(one_layer)

    @pl.when(ranked)
    def _():
        @pl.when(n_below < ns - 1)
        def _():
            pl.semaphore_wait(ok_slab, ns - 1 - n_below)

        @pl.loop(s + 1, ns)
        def _(peer):
            top_copy(peer).start()

        for copy, peer, exists in near:
            pl.when(exists & is_above(peer))(copy.start)

    @pl.when(flowing)
    def _():
        all_tops.wait_recv()
        for j in range(ns):
            cp_stage[j : j + 1, :] = cp_stage[j : j + 1, :] * top_rows(j, slice(R, R + 1))

    early_flow(flowing, 1)
    pl.loop(jnp.where(patient, nz, middle), nz)(one_layer)

    for c in range(H // 8):
        rows = slice(c * 8, c * 8 + 8)
        out[nz - 1, rows, :] = (
            out[nz - 1, rows, :]
            + sa[nz, rows, :] * v_s[nz, rows, :]
            + sb[nz, rows, :] * (1.0 - s_s[nz, rows, :])
        )

    def parts(ref):
        return [ref[f * nz : f * nz + nz, :] for f in range(4)]

    def edge_state(raw):
        a, b, _, _ = half_state(*raw)
        return raw[0], raw[1], a, b

    def outside(exists, raw):
        return [jnp.where(exists, x, 0.0) for x in edge_state(raw)]

    early_rows(early_down, 1)
    if half != 1:
        early_rows((t == 1) | (t == half - 1), 0)

    for copy in col_copies:
        copy.wait_recv()
    ft[...] = jnp.zeros(ft.shape, jnp.float32)
    ft[pl.ds(1, nz, stride=2), :] = face(
        *edge_state(parts(col_l)), *outside(s > 0, parts(rcol_l))
    )
    ft[pl.ds(0, nz, stride=2), :] = face(
        *edge_state(parts(col_r)), *outside(s < ns - 1, parts(rcol_r))
    )
    turned = ft[...].T
    rim_lane = (lane == 0) | (lane == W - 1)
    for layer in range(nz):
        for c in range(H // 8):
            rows = slice(c * 8, c * 8 + 8)
            x = pltpu.roll(turned[rows], W - (2 * layer + 1), 1)
            out[layer, rows, :] = out[layer, rows, :] + jnp.where(rim_lane, x, 0.0)

    pl.when(jnp.logical_not(flowing))(all_tops.wait_recv)

    @pl.when(early_up & (s == 0))
    def _():
        for j in range(ns):
            cm_stage[j : j + 1, :] = cm_stage[j : j + 1, :] * top_rows(j, slice(1, 2))

    @pl.when(s > 0)
    def _():
        slab_coefs[1].wait_recv()
        for j in range(ns):
            c_xp[j, 0:1, :] = rcp[j : j + 1, :]

    @pl.when(s < ns - 1)
    def _():
        slab_coefs[0].wait_recv()
        for j in range(ns):
            c_xm[j, R - 1 : R, :] = rcm[j : j + 1, :]

    small_lane = lax.broadcasted_iota(jnp.int32, (R, W), 1)
    first, last = small_lane == 0, small_lane == W - 1
    nil = jnp.zeros((R, W), jnp.float32)
    prev_plus = nil
    own = [top_rows(j, slice(1, R + 1)) for j in range(ns)]
    minus = [pltpu.roll(c_ym[j] * own[j], W - 1, 1) for j in range(ns)] + [nil]
    for j in range(ns):
        plus = pltpu.roll(c_yp[j] * own[j], 1, 1)
        surf[:, j * W : j * W + W] = (
            c_all[j] * own[j]
            - c_xp[j] * top_rows(j, slice(0, R))
            - c_xm[j] * top_rows(j, slice(2, R + 2))
            - jnp.where(first, prev_plus, plus)
            - jnp.where(last, minus[j + 1], minus[j])
        )
        prev_plus = plus

    early_rows(t == half, 0)
    early_flow(early_up & (s == 0), 0)

    def add_rows(exists, copy, own, theirs, row):
        @pl.when(exists)
        def _():
            copy.wait_recv()
            flux = face(*edge_state(parts(own)), *edge_state(parts(theirs)))
            for layer in range(nz):
                out[layer, row : row + 1, :] = (
                    out[layer, row : row + 1, :] + flux[layer : layer + 1]
                )

        @pl.when(jnp.logical_not(exists))
        def _():
            v, suction, a, b = edge_state(parts(own))
            flux = a * v - b * suction
            for layer in range(nz):
                out[layer, row : row + 1, :] = (
                    out[layer, row : row + 1, :] + flux[layer : layer + 1]
                )

    add_rows(t < nt - 1, row_copies[0], row_dn, rrow_dn, H - 1)
    add_rows(t > 0, row_copies[1], row_up, rrow_up, 0)

    def add_flow(early, late, copy, arrived, row):
        @pl.when(late)
        def _():
            copy.wait_recv()
            for j in range(ns):
                cols = slice(j * W, j * W + W)
                surf[row : row + 1, cols] = surf[row : row + 1, cols] - arrived[j : j + 1, :]

        @pl.when(early)
        def _():
            copy.wait_recv()

            all_rims.wait_recv()
            for j in range(ns):
                cols = slice(j * W, j * W + W)
                surf[row : row + 1, cols] = surf[row : row + 1, cols] - arrived[j : j + 1, :] * rim[j]

    at_end, at_start = s == ns - 1, s == 0
    add_flow(early_down & at_end, late_down & at_end, tile_flows[0], rcm, R - 1)
    add_flow(early_up & at_start, late_up & at_start, tile_flows[1], rcp, 0)

    for copy in col_copies:
        copy.wait_send()
    for side, exists in ((0, t > 0), (1, t < nt - 1)):

        @pl.when(exists)
        def _(side=side):
            row_copies[side].wait_send()

    for side, exists in ((0, late_up), (1, late_down)):

        @pl.when(exists)
        def _(side=side):
            rims[side].wait_send()

    @pl.when((s > 0) | (t > 0))
    def _():
        slab_coefs[0].wait_send()

    @pl.when((s < ns - 1) | (t < nt - 1))
    def _():
        slab_coefs[1].wait_send()

    all_tops.wait_send()


def per_device(nt, ns, *args):
    nz, H, _ = args[0].shape
    R = args[5].shape[0]
    f32 = jnp.float32
    vm = pltpu.VMEM
    dma = pltpu.SemaphoreType.DMA
    anywhere = pl.BlockSpec(memory_space=pl.ANY)
    return pl.pallas_call(
        functools.partial(kernel, nt, ns, nz, H, R),
        out_shape=(
            vm((nz, H, W), f32),
            vm((R, ns * W), f32),
        ),
        in_specs=[anywhere] * 11,
        out_specs=(pl.BlockSpec(memory_space=pltpu.VMEM),) * 2,
        scratch_shapes=[
            vm((nz + 2, H, W), f32),
            vm((nz + 2, H, W), f32),
            vm((nz, H, W), f32),
            vm((nz, H, W), f32),
            vm((nz, H, W), f32),
            vm((nz + 2, H, W), f32),
            vm((nz + 2, H, W), f32),
            vm((R, ns * W), f32),
            vm((R, ns * W), f32),
            vm((R, ns * W), f32),
            vm((R, ns * W), f32),
            vm((R, ns * W), jnp.int32),
            vm((R, ns * W), jnp.int32),
            vm((ns, R, W), f32),
            vm((ns, R, W), f32),
            vm((ns, R, W), f32),
            vm((ns, R, W), f32),
            vm((ns, R, W), f32),
            vm((ns, R + 2, W), f32),
            vm((ns, R + 2, W), f32),
            vm((2, 1, W), f32),
            vm((ns, 1, W), f32),
            vm((ns, W), f32),
            vm((ns, W), f32),
            vm((ns, W), f32),
            vm((ns, W), f32),
            vm((4 * nz, W), f32),
            vm((4 * nz, W), f32),
            vm((4 * nz, W), f32),
            vm((4 * nz, W), f32),
            vm((4 * nz, H), f32),
            vm((4 * nz, H), f32),
            vm((4 * nz, H), f32),
            vm((4 * nz, H), f32),
            vm((W, H), f32),
            vm((W, H), f32),
            dma((11,)),
            dma((1,)),
            dma((1,)),
            dma((2,)),
            dma((1,)),
            dma((2,)),
            dma((2,)),
            dma((4,)),
            dma((4,)),
            pltpu.SemaphoreType.REGULAR((2,)),
            pltpu.SemaphoreType.REGULAR((2,)),
            pltpu.SemaphoreType.REGULAR,
        ],
        compiler_params=pltpu.CompilerParams(
            collective_id=0, has_side_effects=True, vmem_limit_bytes=56 * 1024 * 1024
        ),
    )(*args)


def solution(mesh):
    cells = P(None, "tile", "slab")
    surface = P(("tile", "slab"), None)
    return jax.shard_map(
        functools.partial(per_device, mesh.shape["tile"], mesh.shape["slab"]),
        mesh=mesh,
        in_specs=(cells,) * 5 + (surface,) * 6,
        out_specs=(cells, surface),
        check_vma=False,
    )
```
